32 devices in a mesh: lat: 4 (over x, core), lon: 8 (over z, y).
Axes of the slice: x: 2, y: 2, z: 4, core: 2. Of those that a mesh axis runs over, the one named last changes fastest.
Arguments:
- state: float32 [32, 144, 192], P('lat', 'lon'), may hold values from -6 to 6
- courant_east: float32 [32, 144, 192], P('lat', 'lon'), may hold values from -0.9 to 0.9
- courant_north: float32 [32, 144, 192], P('lat', 'lon'), may hold values from -0.9 to 0.9
- cutoff: int32 [32], P('lat'), may hold values from 1 to 67, as said below
- filter_mask: int32 [32], P('lat'), may hold values from 0 to 1, as said below
Outputs:
- advanced: float32 [32, 144, 192], P('lat', 'lon')
The draws below stay inside these ranges and needn't reach their ends.
Inputs may be any that keep to these rules, and one draw needn't show every extreme that they name: Row j's cutoff is at most 18 + 53 * d // 16, where d = min(j, 31 - j), and equals that bound on the two rows with d = 15; the two rows with d = 0 have cutoff 1. filter_mask is 0 on every row j with min(j, 31 - j) >= 8, and 1 on row 0.
All inputs are finite; a program needn't handle non-finite values.
Results may differ from the reference program's by a relative error of at most 0.00012.
Values sent between devices are 32-bit elements; how exact they have to be, the bound alone decides.
A program may use at most 64 MiB of HBM per device.

```python
import math
import jax
import jax.numpy as jnp

NLAT = 32
NLON = 144
COMP = 192


def draw_cutoff(key, part):
    row_ids = jnp.arange(NLAT, dtype=jnp.int32)
    to_pole = jnp.minimum(row_ids, NLAT - 1 - row_ids)
    ceiling = NLON // 8 + (NLON // 2 - 1 - NLON // 8) * to_pole // (NLAT // 2)
    drawn = jax.random.randint(jax.random.fold_in(key, 11), (NLAT,), 1, ceiling + 1, dtype=jnp.int32)
    drawn = jnp.where(to_pole == NLAT // 2 - 1, ceiling, drawn)
    return jnp.where(to_pole == 0, jnp.ones_like(drawn), drawn)


def draw_filter_mask(key, part):
    row_ids = jnp.arange(NLAT, dtype=jnp.int32)
    to_pole = jnp.minimum(row_ids, NLAT - 1 - row_ids)
    coins = jax.random.randint(jax.random.fold_in(key, 23), (NLAT,), 0, 2, dtype=jnp.int32)
    inside = jnp.where(to_pole < NLAT // 4, coins, jnp.zeros_like(coins))
    return jnp.where(row_ids == 0, jnp.ones_like(inside), inside)


def shard_levels(own_key, dims, pieces, smallest, high):
    factor_of = 1.0
    for axis_at, shards_of in pieces:
        draws = jax.random.uniform(jax.random.fold_in(jax.random.fold_in(own_key, 6), axis_at), (shards_of,), jnp.float32, smallest / len(pieces), high / len(pieces))
        factor_of = factor_of * jnp.repeat(jnp.exp(draws), dims[axis_at] // shards_of).reshape((-1,) + (1,) * (len(dims) - 1 - axis_at))
    return factor_of


def scatter_about(stream_key, shape, deviation, bound, split=(), held_as=jnp.bfloat16):
    array = jax.random.normal(stream_key, shape, jnp.float32) * deviation
    if len(split) > 0:
        array = shard_levels(stream_key, shape, split, -0.22, 0.18) * array
    return jnp.clip(array, min=-bound, max=bound).astype(held_as)


def setup_inputs(seed: int = 0) -> dict:
    key_of = jax.random.split(jax.random.key(seed), 6)
    return {
        "state": scatter_about(key_of[0], (NLAT, NLON, COMP), 1.0, 6.0, ((0, 4), (1, 8)), jnp.float32),
        "courant_east": jnp.clip(jax.random.uniform(key_of[1], (NLAT, NLON, COMP), jnp.float32, -0.9, 0.9) * shard_levels(key_of[1], (NLAT, NLON, COMP), ((0, 4), (1, 8)), -0.4, 0.0), -0.9, 0.9),
        "courant_north": jnp.clip(jax.random.uniform(key_of[2], (NLAT, NLON, COMP), jnp.float32, -0.9, 0.9) * shard_levels(key_of[2], (NLAT, NLON, COMP), ((0, 4), (1, 8)), -0.4, 0.0), -0.9, 0.9),
        "cutoff": draw_cutoff(jax.random.fold_in(key_of[5], 71), 0),
        "filter_mask": draw_filter_mask(jax.random.fold_in(key_of[5], 71), 0),
    }


def face_flux(far_lo, near_lo, near_hi, far_hi, courant):
    centred = (7.0 * (near_lo + near_hi) - (far_lo + far_hi)) / 12.0
    return courant * centred - 0.5 * jnp.abs(courant) * (near_hi - near_lo)


def reference(state, courant_east, courant_north, cutoff, filter_mask):
    spectra = jnp.fft.rfft(state, axis=1)
    waves = jnp.arange(NLON // 2 + 1, dtype=jnp.int32)
    allowed = waves[None, :] <= cutoff[:, None]
    filtered = jnp.fft.irfft(jnp.where(allowed[:, :, None], spectra, 0.0), n=NLON, axis=1).astype(jnp.float32)
    smooth = jnp.where(filter_mask[:, None, None] == 1, filtered, state)
    south = jnp.roll(smooth[:2][::-1], NLON // 2, axis=1)
    north = jnp.roll(smooth[::-1][:2], NLON // 2, axis=1)
    merid_p = jnp.concatenate([south, smooth, north], axis=0)
    zonal_p = jnp.concatenate([smooth[:, -2:], smooth, smooth[:, :2]], axis=1)
    zonal_c = jnp.concatenate([courant_east[:, -1:], courant_east], axis=1)
    east = face_flux(zonal_p[:, 0:NLON + 1], zonal_p[:, 1:NLON + 2], zonal_p[:, 2:NLON + 3], zonal_p[:, 3:NLON + 4], zonal_c)
    zonal = -(east[:, 1:] - east[:, :-1])
    merid_c = jnp.concatenate([jnp.zeros_like(courant_north[:1]), courant_north], axis=0)
    north_flux = face_flux(merid_p[0:NLAT + 1], merid_p[1:NLAT + 2], merid_p[2:NLAT + 3], merid_p[3:NLAT + 4], merid_c)
    face_rows = jnp.arange(-1, NLAT, dtype=jnp.int32)
    cos_face = jnp.sin(jnp.minimum(face_rows + 1, NLAT - 1 - face_rows).astype(jnp.float32) * (math.pi / NLAT))
    cell_rows = face_rows[1:]
    cos_cell = jnp.sin((jnp.minimum(cell_rows, NLAT - 1 - cell_rows).astype(jnp.float32) + 0.5) * (math.pi / NLAT))
    weighted = cos_face[:, None, None] * north_flux
    meridional = -(weighted[1:] - weighted[:-1]) / cos_cell[:, None, None]
    return smooth + zonal + meridional
```

```python
import functools
import math

import jax
import jax.numpy as jnp
import numpy as np
from jax import lax
from jax.experimental import pallas as pl
from jax.experimental.pallas import tpu as pltpu
from jax.sharding import PartitionSpec as P

HIGHEST = lax.Precision.HIGHEST


def passed_along(block, axis, distance):
    devices = range(lax.axis_size(axis))
    route = [((i - distance) % len(devices), i) for i in devices]
    return lax.ppermute(block, axis, route)


def padded_2(value, sides, width):
    for axis, dim in sides:
        count, length = (lax.axis_size(axis), value.shape[dim])
        up = [(i, (i + 1) % count) for i in range(count)]
        down = [(j, i) for i, j in up]
        last = lax.slice_in_dim(value, length - width, length, axis=dim)
        initial = lax.slice_in_dim(value, 0, width, axis=dim)
        before = lax.ppermute(last, axis, up)
        after = lax.ppermute(initial, axis, down)
        value = jnp.concatenate([before, value, after], axis=dim)
    return value


def face_flux(far_lo, near_lo, near_hi, far_hi, courant):
    centred = (7.0 * (near_lo + near_hi) - (far_lo + far_hi)) / 12.0
    return courant * centred - 0.5 * jnp.abs(courant) * (near_hi - near_lo)


def build_table(n_full, n_half):
    points = jnp.arange(n_full, dtype=jnp.int32)
    waves = jnp.arange(n_half, dtype=jnp.int32)
    phase = points[:, None] * waves[None, :] % n_full
    angle = phase.astype(jnp.float32) * (2.0 * math.pi / n_full)
    return jnp.concatenate([jnp.cos(angle), jnp.sin(angle)], axis=1)


def pole_rows(field):
    return jnp.concatenate([field[:2][::-1], field[::-1][:2]], axis=0)


def send_rows(field):
    return lax.all_to_all(field, "lon", split_axis=2, concat_axis=1, tiled=True)


def return_rows(merged, lon_count):
    smooth = lax.all_to_all(merged, "lon", split_axis=1, concat_axis=2, tiled=True)
    partner = passed_along(pole_rows(smooth), "lon", lon_count // 2)
    return (smooth, partner)


def local(state, courant_east, courant_north, cutoff, filter_mask):
    n_rows, n_cols, n_comp = state.shape
    lon_count = lax.axis_size("lon")
    lat_count = lax.axis_size("lat")
    lat_index = lax.axis_index("lat")
    n_full = n_cols * lon_count
    n_half = n_full // 2 + 1
    n_lat = n_rows * lat_count
    fourier = build_table(n_full, n_half)
    waves = jnp.arange(n_half, dtype=jnp.int32)
    weights = jnp.where((waves == 0) | (waves == n_half - 1), 1.0 / n_full, 2.0 / n_full).astype(
        jnp.float32
    )
    row_lines = send_rows(state)
    kept = jnp.where(waves[None, :] <= cutoff[:, None], weights[None, :], 0.0)
    kept_both = jnp.concatenate([kept, kept], axis=1)
    coeffs = lax.dot_general(
        row_lines, fourier, (((1,), (0,)), ((), ())), precision=lax.Precision.HIGHEST
    )
    coeffs = coeffs * kept_both[:, None, :]
    synth = lax.dot_general(
        coeffs, fourier, (((2,), (1,)), ((), ())), precision=lax.Precision.HIGHEST
    )
    filtered = jnp.transpose(synth, (0, 2, 1))
    merged = jnp.where(filter_mask[:, None, None] == 1, filtered, row_lines)
    smooth, partner = return_rows(merged, lon_count)
    stacked = jnp.stack([smooth, courant_east, courant_north])
    padded = padded_2(stacked, (("lat", 1), ("lon", 2)), 2)
    zonal_p = padded[0, 2:-2]
    zonal_c = padded[1, 2:-2]
    east = face_flux(
        zonal_p[:, 0 : n_cols + 1],
        zonal_p[:, 1 : n_cols + 2],
        zonal_p[:, 2 : n_cols + 3],
        zonal_p[:, 3 : n_cols + 4],
        zonal_c[:, 1 : n_cols + 2],
    )
    zonal = -(east[:, 1:] - east[:, :-1])
    merid_p = padded[0, :, 2:-2]
    south = jnp.where(lat_index == 0, partner[:2], merid_p[:2])
    north = jnp.where(lat_index == lat_count - 1, partner[2:], merid_p[-2:])
    merid_p = jnp.concatenate([south, merid_p[2:-2], north], axis=0)
    merid_c = padded[2, :, 2:-2]
    north_flux = face_flux(
        merid_p[0 : n_rows + 1],
        merid_p[1 : n_rows + 2],
        merid_p[2 : n_rows + 3],
        merid_p[3 : n_rows + 4],
        merid_c[1 : n_rows + 2],
    )
    face_rows = lat_index * n_rows + jnp.arange(-1, n_rows, dtype=jnp.int32)
    cos_face = jnp.sin(
        jnp.minimum(face_rows + 1, n_lat - 1 - face_rows).astype(jnp.float32) * (math.pi / n_lat)
    )
    cell_rows = face_rows[1:]
    cos_cell = jnp.sin(
        (jnp.minimum(cell_rows, n_lat - 1 - cell_rows).astype(jnp.float32) + 0.5)
        * (math.pi / n_lat)
    )
    weighted = cos_face[:, None, None] * north_flux
    meridional = -(weighted[1:] - weighted[:-1]) / cos_cell[:, None, None]
    return smooth + zonal + meridional


def spread(n_cols):
    return -(-(n_cols + 4) // 8) * 8


def wave_tables(n_cols, lon_count, n_lat):
    n_full, wide = n_cols * lon_count, spread(n_cols)
    low = n_full // 8
    n_waves = low + (n_full // 2 - 1 - low) * (n_lat // 4 - 1) // (n_lat // 2) + 1
    lanes = -(-2 * n_waves // 128) * 128
    place = np.arange(wide)
    offset = np.where(place < n_cols + 2, place, place - wide)
    column = (np.arange(lon_count)[:, None] * n_cols + offset[None, :]).reshape(-1) % n_full
    angle = column[:, None] * np.arange(n_waves)[None, :] % n_full * (2.0 * np.pi / n_full)
    table = np.zeros((lon_count * wide, lanes), np.float64)
    table[:, : 2 * n_waves] = np.concatenate([np.cos(angle), np.sin(angle)], axis=1)
    given = np.tile((place < n_cols + 2) | (place >= wide - 2), lon_count)
    own = np.tile(place < n_cols, lon_count)
    synth = np.where(given[:, None], table, 0.0).astype(np.float32)
    analyse = np.where(own[:, None], table, 0.0).T.astype(np.float32)
    return synth, analyse, n_waves


def fused_kernel(
    n_waves, cut_ref, mask_ref, st_ref, ce_ref, cn_ref, t1_ref, t2_ref, out_ref,
    blocks, lines, synth, ext, ce_wide, to_east, to_west, from_west, from_east, cn_south,
    send_a, recv_a, send_b, recv_rows, send_c, send_raw, recv_raw, send_cn, recv_cn,
    send_edge, recv_edge,
):
    n_rows, n_cols, n_comp = st_ref.shape
    wide = blocks.shape[1]
    n_full = n_rows * n_cols
    lat_count, lon_count = lax.axis_size("lat"), n_rows
    n_lat = n_rows * lat_count
    a, i = lax.axis_index("lat"), lax.axis_index("lon")
    southern = a < 2
    polar = jnp.logical_or(a == 0, a == lat_count - 1)
    other = jnp.where(southern, 1 - a, 5 - a)
    first_edge = jnp.where(southern, n_rows - 2, 0)
    first_pole = jnp.where(southern, 0, n_rows - 2)
    is_edge = jnp.logical_and(i >= first_edge, i < first_edge + 2)
    is_pole = jnp.logical_and(i >= first_pole, i < first_pole + 2)
    east_i, west_i = lax.rem(i + 1, lon_count), lax.rem(i + lon_count - 1, lon_count)
    half = lon_count // 2

    def remote(src, dst, send, recv, lat, lon):
        return pltpu.make_async_remote_copy(
            src_ref=src, dst_ref=dst, send_sem=send, recv_sem=recv,
            device_id=(lat, lon), device_id_type=pl.DeviceIdType.MESH,
        )

    barrier = pltpu.get_barrier_semaphore()

    def greet(lat, lon):
        pl.semaphore_signal(
            barrier, inc=1, device_id=(lat, lon), device_id_type=pl.DeviceIdType.MESH
        )

    @pl.when(polar)
    def _():
        for step in range(1, lon_count):
            greet(a, lax.rem(i + step, lon_count))

        @pl.when(is_edge)
        def _():
            for lon in range(lon_count):
                greet(other, lon)

        @pl.when(jnp.logical_not(is_edge))
        def _():
            greet(other, i)

    @pl.when(jnp.logical_not(polar))
    def _():
        greet(a, east_i)
        greet(a, west_i)
        greet(3 - a, i)
        greet(other, first_edge)
        greet(other, first_edge + 1)

        @pl.when(jnp.logical_not(is_edge))
        def _():
            greet(other, i)

    zero = jnp.zeros((n_rows, wide - n_cols // 8 * 8, n_comp), jnp.float32)
    blocks[:, n_cols // 8 * 8 :, :] = zero
    blocks[:, :n_cols, :] = st_ref[...]
    ce_wide[:, n_cols // 8 * 8 :, :] = zero
    ce_wide[:, :n_cols, :] = ce_ref[...]
    to_east[2] = ce_ref[:, n_cols - 1, :]

    @pl.when(jnp.logical_not(polar))
    def _():
        to_east[0] = st_ref[:, n_cols - 2, :]
        to_east[1] = st_ref[:, n_cols - 1, :]
        to_west[0] = st_ref[:, 0, :]
        to_west[1] = st_ref[:, 1, :]

    @pl.when(polar)
    def _():
        lines[i] = blocks[i]

    @pl.when(a == 0)
    def _():
        cn_south[...] = jnp.zeros_like(cn_south)

    @pl.when(polar)
    def _():
        pl.semaphore_wait(barrier, lon_count - 1 + jnp.where(is_edge, lon_count, 1))

    @pl.when(jnp.logical_not(polar))
    def _():
        pl.semaphore_wait(barrier, 5 + jnp.where(is_edge, 0, 1))

    def row_copy(step):
        to = lax.rem(i + step, lon_count)
        return remote(blocks.at[to], lines.at[i], send_a.at[step], recv_a.at[step], a, to)

    cn_copy = remote(cn_ref.at[n_rows - 1], cn_south, send_cn, recv_cn, a + 1, i)
    edge_ce = remote(
        to_east.at[2], from_west.at[2], send_edge.at[0], recv_edge.at[0], a, east_i
    )
    edge_east = remote(to_east, from_west, send_edge.at[0], recv_edge.at[0], a, east_i)
    edge_west = remote(to_west, from_east, send_edge.at[1], recv_edge.at[1], a, west_i)
    raw_south = remote(
        blocks.at[pl.ds(0, 2)], ext.at[pl.ds(n_rows + 2, 2)],
        send_raw.at[0], recv_raw.at[1], a - 1, i,
    )
    raw_north = remote(
        blocks.at[pl.ds(n_rows - 2, 2)], ext.at[pl.ds(0, 2)],
        send_raw.at[1], recv_raw.at[0], a + 1, i,
    )

    @pl.when(polar)
    def _():
        for step in range(1, lon_count):
            row_copy(step).start()
        edge_ce.start()

    @pl.when(jnp.logical_not(polar))
    def _():
        edge_east.start()
        edge_west.start()
        raw_south.start()
        raw_north.start()

    @pl.when(a < lat_count - 1)
    def _():
        cn_copy.start()

    def line_copy(step):
        to = lax.rem(i + step, lon_count)
        return remote(
            synth.at[to], ext.at[i + 2], send_b.at[step], recv_rows.at[i + 2], a, to
        )

    pole_slot = jnp.where(southern, 1 - i, n_rows * 2 + 1 - i)
    edge_slot = jnp.where(southern, i - (n_rows - 2), n_rows + 2 + i)

    def pole_copy(step):
        to = lax.rem(i + step, lon_count)
        return remote(
            synth.at[lax.rem(to + half, lon_count)], ext.at[pole_slot],
            send_c.at[step], recv_rows.at[pole_slot], a, to,
        )

    def edge_copy(lon):
        return remote(
            synth.at[lon], ext.at[edge_slot], send_c.at[lon], recv_rows.at[edge_slot], other, lon
        )

    def slot_wait(slot):
        remote(blocks.at[0], ext.at[slot], send_b.at[0], recv_rows.at[slot], a, east_i).wait_recv()

    @pl.when(polar)
    def _():
        lane = lax.broadcasted_iota(jnp.int32, (1, t1_ref.shape[1]), 1)
        wave = jnp.where(lane < n_waves, lane, lane - n_waves)
        kept = jnp.where(wave == 0, 1.0 / n_full, 2.0 / n_full).astype(jnp.float32)
        kept = jnp.where(wave <= cut_ref[i], kept, 0.0)
        weights = lax.dot_general(
            t1_ref[...] * kept, t2_ref[...], (((1,), (0,)), ((), ())), precision=HIGHEST,
            preferred_element_type=jnp.float32,
        )
        size = lon_count * wide
        dim = (lon_count, wide, 1)
        place = lax.broadcasted_iota(jnp.int32, dim, 1)
        at = lax.broadcasted_iota(jnp.int32, dim, 0) * n_cols
        at = at + jnp.where(place < n_cols + 2, place, place - wide)
        at = jnp.where(at < 0, at + n_full, jnp.where(at >= n_full, at - n_full, at))
        at = jnp.where((place >= n_cols + 2) & (place < wide - 2), -1, at).reshape(size, 1)
        lane = lax.broadcasted_iota(jnp.int32, (1, size), 1)
        start = jnp.zeros((1, size), jnp.int32)
        for q in range(1, lon_count):
            start = start + jnp.where(lane >= q * wide, 1, 0)
        inner = lane - start * wide
        source = jnp.where(inner < n_cols, start * n_cols + inner, -2)
        weights = jnp.where(mask_ref[i] == 1, weights, jnp.where(at == source, 1.0, 0.0))
        w_hi = weights.astype(jnp.bfloat16)
        w_lo = (weights - w_hi.astype(jnp.float32)).astype(jnp.bfloat16)
        for step in range(1, lon_count):
            row_copy(step).wait_recv()
        line = lines[...].reshape(size, n_comp)
        l_hi = line.astype(jnp.bfloat16)
        l_lo = (line - l_hi.astype(jnp.float32)).astype(jnp.bfloat16)

        def times(left, right):
            return lax.dot_general(
                left, right, (((1,), (0,)), ((), ())), preferred_element_type=jnp.float32
            )

        smooth = times(w_hi, l_hi) + (times(w_hi, l_lo) + times(w_lo, l_hi))
        synth[...] = smooth.reshape(lon_count, wide, n_comp)
        for step in range(1, lon_count):
            line_copy(step).start()

        @pl.when(is_edge)
        def _():
            for lon in range(lon_count):
                edge_copy(lon).start()

        @pl.when(is_pole)
        def _():
            for step in range(1, lon_count):
                pole_copy(step).start()
            ext[pole_slot] = synth[lax.rem(i + half, lon_count)]

        ext[i + 2] = synth[i]

    @pl.when(jnp.logical_not(polar))
    def _():
        edge_east.wait_recv()
        edge_west.wait_recv()
        place = lax.broadcasted_iota(jnp.int32, (wide, 1), 0)
        for r in range(n_rows):
            row = blocks[r]
            row = jnp.where(place == wide - 2, from_west[0, r : r + 1, :], row)
            row = jnp.where(place == wide - 1, from_west[1, r : r + 1, :], row)
            row = jnp.where(place == n_cols, from_east[0, r : r + 1, :], row)
            row = jnp.where(place == n_cols + 1, from_east[1, r : r + 1, :], row)
            ext[r + 2] = row

    @pl.when(polar)
    def _():
        edge_ce.wait_recv()

    @pl.when(a > 0)
    def _():
        cn_copy.wait_recv()

    @pl.when(southern)
    def _():
        raw_south.wait_recv()

    @pl.when(jnp.logical_not(southern))
    def _():
        raw_north.wait_recv()

    @pl.when(polar)
    def _():
        for step in range(1, lon_count):
            slot_wait(lax.rem(i + step, lon_count) + 2)
        for m in range(2):
            owner = first_pole + m
            slot = jnp.where(southern, 1 - m, n_rows + 3 - m)

            @pl.when(owner != i)
            def _():
                slot_wait(slot)

    @pl.when(jnp.logical_not(polar))
    def _():
        for m in range(2):
            slot_wait(jnp.where(southern, m, n_rows + 2 + m))

    def by_lat(values):
        chosen = jnp.float32(values[0])
        for lat in range(1, lat_count):
            chosen = jnp.where(a == lat, jnp.float32(values[lat]), chosen)
        return chosen

    def flux(far_lo, near_lo, near_hi, far_hi, courant):
        centred = (7.0 * (near_lo + near_hi) - (far_lo + far_hi)) * (1.0 / 12.0)
        return courant * centred - 0.5 * jnp.abs(courant) * (near_hi - near_lo)

    place = lax.broadcasted_iota(jnp.int32, (wide, 1), 0)
    below = None
    for f in range(-1, n_rows):
        faces = [lat * n_rows + f for lat in range(lat_count)]
        cos_face = by_lat([math.sin(min(g + 1, n_lat - 1 - g) * math.pi / n_lat) for g in faces])
        courant = cn_south[...] if f < 0 else cn_ref[f]
        stencil = [ext[f + 1 + t, :n_cols, :] for t in range(4)]
        weighted = cos_face * flux(*stencil, courant)
        if f >= 0:
            row = ext[f + 2]
            u = jnp.where(place == wide - 1, from_west[2, f : f + 1, :], ce_wide[f])
            east = flux(
                pltpu.roll(row, 1, 0), row, pltpu.roll(row, wide - 1, 0),
                pltpu.roll(row, wide - 2, 0), u,
            )
            zonal = -(east - pltpu.roll(east, 1, 0))
            per_cos = by_lat(
                [1.0 / math.sin((min(g, n_lat - 1 - g) + 0.5) * math.pi / n_lat) for g in faces]
            )
            out_ref[f] = (row + zonal)[:n_cols] - (weighted - below) * per_cos
        below = weighted

    @pl.when(polar)
    def _():
        for step in range(1, lon_count):
            row_copy(step).wait_send()
            line_copy(step).wait_send()
        edge_ce.wait_send()

        @pl.when(is_edge)
        def _():
            for lon in range(lon_count):
                edge_copy(lon).wait_send()

        @pl.when(is_pole)
        def _():
            for step in range(1, lon_count):
                pole_copy(step).wait_send()

    @pl.when(jnp.logical_not(polar))
    def _():
        edge_east.wait_send()
        edge_west.wait_send()
        raw_south.wait_send()
        raw_north.wait_send()

    @pl.when(a < lat_count - 1)
    def _():
        cn_copy.wait_send()


def local_fused(state, courant_east, courant_north, cutoff, filter_mask):
    n_rows, n_cols, n_comp = state.shape
    wide = spread(n_cols)
    synth, analyse, n_waves = wave_tables(n_cols, n_rows, n_rows * 4)
    vmem = pl.BlockSpec(memory_space=pltpu.VMEM)
    smem = pl.BlockSpec(memory_space=pltpu.SMEM)
    block = pltpu.VMEM((n_rows, wide, n_comp), jnp.float32)
    dma = pltpu.SemaphoreType.DMA
    edge = lambda count: pltpu.VMEM((count, n_rows, n_comp), jnp.float32)
    return pl.pallas_call(
        functools.partial(fused_kernel, n_waves),
        out_shape=jax.ShapeDtypeStruct(state.shape, jnp.float32),
        in_specs=[smem, smem] + [vmem] * 5,
        out_specs=vmem,
        scratch_shapes=[
            block, block, block,
            pltpu.VMEM((n_rows + 4, wide, n_comp), jnp.float32),
            block, edge(3), edge(2), edge(3), edge(2),
            pltpu.VMEM((n_cols, n_comp), jnp.float32),
            dma((n_rows,)), dma((n_rows,)), dma((n_rows,)), dma((n_rows + 4,)), dma((n_rows,)),
            dma((2,)), dma((2,)), dma, dma, dma((2,)), dma((2,)),
        ],
        compiler_params=pltpu.CompilerParams(
            collective_id=0, has_side_effects=True, vmem_limit_bytes=32 * 1024 * 1024
        ),
    )(cutoff, filter_mask, state, courant_east, courant_north, synth, analyse)


def solution(mesh):
    placed = (
        P("lat", "lon", None),
        P("lat", "lon", None),
        P("lat", "lon", None),
        P("lat"),
        P("lat"),
    )

    def dispatch(*arrays):
        n_rows = arrays[0].shape[0]
        row_each = mesh.shape["lat"] == 4 and mesh.shape["lon"] == n_rows and n_rows >= 8
        return (local_fused if row_each else local)(*arrays)

    return jax.shard_map(
        dispatch, mesh=mesh, in_specs=placed, out_specs=P("lat", "lon", None), check_vma=False
    )
```

```python
import functools
import math

import jax
import jax.numpy as jnp
import numpy as np
from jax import lax
from jax.experimental import pallas as pl
from jax.experimental.pallas import tpu as pltpu
from jax.sharding import PartitionSpec as P

HIGHEST = lax.Precision.HIGHEST


def passed_along(block, axis, distance):
    devices = range(lax.axis_size(axis))
    route = [((i - distance) % len(devices), i) for i in devices]
    return lax.ppermute(block, axis, route)


def padded_2(value, sides, width):
    for axis, dim in sides:
        count, length = (lax.axis_size(axis), value.shape[dim])
        up = [(i, (i + 1) % count) for i in range(count)]
        down = [(j, i) for i, j in up]
        last = lax.slice_in_dim(value, length - width, length, axis=dim)
        initial = lax.slice_in_dim(value, 0, width, axis=dim)
        before = lax.ppermute(last, axis, up)
        after = lax.ppermute(initial, axis, down)
        value = jnp.concatenate([before, value, after], axis=dim)
    return value


def face_flux(far_lo, near_lo, near_hi, far_hi, courant):
    centred = (7.0 * (near_lo + near_hi) - (far_lo + far_hi)) / 12.0
    return courant * centred - 0.5 * jnp.abs(courant) * (near_hi - near_lo)


def build_table(n_full, n_half):
    points = jnp.arange(n_full, dtype=jnp.int32)
    waves = jnp.arange(n_half, dtype=jnp.int32)
    phase = points[:, None] * waves[None, :] % n_full
    angle = phase.astype(jnp.float32) * (2.0 * math.pi / n_full)
    return jnp.concatenate([jnp.cos(angle), jnp.sin(angle)], axis=1)


def pole_rows(field):
    return jnp.concatenate([field[:2][::-1], field[::-1][:2]], axis=0)


def send_rows(field):
    return lax.all_to_all(field, "lon", split_axis=2, concat_axis=1, tiled=True)


def return_rows(merged, lon_count):
    smooth = lax.all_to_all(merged, "lon", split_axis=1, concat_axis=2, tiled=True)
    partner = passed_along(pole_rows(smooth), "lon", lon_count // 2)
    return (smooth, partner)


def local(state, courant_east, courant_north, cutoff, filter_mask):
    n_rows, n_cols, n_comp = state.shape
    lon_count = lax.axis_size("lon")
    lat_count = lax.axis_size("lat")
    lat_index = lax.axis_index("lat")
    n_full = n_cols * lon_count
    n_half = n_full // 2 + 1
    n_lat = n_rows * lat_count
    fourier = build_table(n_full, n_half)
    waves = jnp.arange(n_half, dtype=jnp.int32)
    weights = jnp.where((waves == 0) | (waves == n_half - 1), 1.0 / n_full, 2.0 / n_full).astype(
        jnp.float32
    )
    row_lines = send_rows(state)
    kept = jnp.where(waves[None, :] <= cutoff[:, None], weights[None, :], 0.0)
    kept_both = jnp.concatenate([kept, kept], axis=1)
    coeffs = lax.dot_general(
        row_lines, fourier, (((1,), (0,)), ((), ())), precision=lax.Precision.HIGHEST
    )
    coeffs = coeffs * kept_both[:, None, :]
    synth = lax.dot_general(
        coeffs, fourier, (((2,), (1,)), ((), ())), precision=lax.Precision.HIGHEST
    )
    filtered = jnp.transpose(synth, (0, 2, 1))
    merged = jnp.where(filter_mask[:, None, None] == 1, filtered, row_lines)
    smooth, partner = return_rows(merged, lon_count)
    stacked = jnp.stack([smooth, courant_east, courant_north])
    padded = padded_2(stacked, (("lat", 1), ("lon", 2)), 2)
    zonal_p = padded[0, 2:-2]
    zonal_c = padded[1, 2:-2]
    east = face_flux(
        zonal_p[:, 0 : n_cols + 1],
        zonal_p[:, 1 : n_cols + 2],
        zonal_p[:, 2 : n_cols + 3],
        zonal_p[:, 3 : n_cols + 4],
        zonal_c[:, 1 : n_cols + 2],
    )
    zonal = -(east[:, 1:] - east[:, :-1])
    merid_p = padded[0, :, 2:-2]
    south = jnp.where(lat_index == 0, partner[:2], merid_p[:2])
    north = jnp.where(lat_index == lat_count - 1, partner[2:], merid_p[-2:])
    merid_p = jnp.concatenate([south, merid_p[2:-2], north], axis=0)
    merid_c = padded[2, :, 2:-2]
    north_flux = face_flux(
        merid_p[0 : n_rows + 1],
        merid_p[1 : n_rows + 2],
        merid_p[2 : n_rows + 3],
        merid_p[3 : n_rows + 4],
        merid_c[1 : n_rows + 2],
    )
    face_rows = lat_index * n_rows + jnp.arange(-1, n_rows, dtype=jnp.int32)
    cos_face = jnp.sin(
        jnp.minimum(face_rows + 1, n_lat - 1 - face_rows).astype(jnp.float32) * (math.pi / n_lat)
    )
    cell_rows = face_rows[1:]
    cos_cell = jnp.sin(
        (jnp.minimum(cell_rows, n_lat - 1 - cell_rows).astype(jnp.float32) + 0.5)
        * (math.pi / n_lat)
    )
    weighted = cos_face[:, None, None] * north_flux
    meridional = -(weighted[1:] - weighted[:-1]) / cos_cell[:, None, None]
    return smooth + zonal + meridional


def spread(n_cols):
    return -(-(n_cols + 4) // 8) * 8


def wave_tables(n_cols, lon_count, n_lat):
    n_full, wide = n_cols * lon_count, spread(n_cols)
    low = n_full // 8
    n_waves = low + (n_full // 2 - 1 - low) * (n_lat // 4 - 1) // (n_lat // 2) + 1
    lanes = -(-2 * n_waves // 128) * 128
    place = np.arange(wide)
    offset = np.where(place < n_cols + 2, place, place - wide)
    column = (np.arange(lon_count)[:, None] * n_cols + offset[None, :]).reshape(-1) % n_full
    angle = column[:, None] * np.arange(n_waves)[None, :] % n_full * (2.0 * np.pi / n_full)
    table = np.zeros((lon_count * wide, lanes), np.float64)
    table[:, : 2 * n_waves] = np.concatenate([np.cos(angle), np.sin(angle)], axis=1)
    given = np.tile((place < n_cols + 2) | (place >= wide - 2), lon_count)
    own = np.tile(place < n_cols, lon_count)
    synth = np.where(given[:, None], table, 0.0).astype(np.float32)
    analyse = np.where(own[:, None], table, 0.0).T.astype(np.float32)
    return synth, analyse, n_waves


def fused_kernel(
    n_waves, cut_in, mask_in, st_in, ce_in, cn_in, t1_in, t2_in, out_ref,
    cut_ref, mask_ref, st_ref, ce_ref, cn_ref, t1_ref, t2_ref, loaded,
    blocks, lines, synth, ext, ce_rows, cn_rows, to_east, to_west, from_west, from_east, cn_south,
    send_a, recv_a, send_b, recv_rows, send_c, send_raw, recv_raw, send_cn, recv_cn,
    send_edge, recv_edge,
):
    n_rows, wide, n_comp = blocks.shape
    n_cols = st_ref.shape[0]
    n_full = n_rows * n_cols
    lat_count, lon_count = lax.axis_size("lat"), n_rows
    n_lat = n_rows * lat_count
    a, i = lax.axis_index("lat"), lax.axis_index("lon")
    southern = a < 2
    polar = jnp.logical_or(a == 0, a == lat_count - 1)
    other = jnp.where(southern, 1 - a, 5 - a)
    first_edge = jnp.where(southern, n_rows - 2, 0)
    first_pole = jnp.where(southern, 0, n_rows - 2)
    is_edge = jnp.logical_and(i >= first_edge, i < first_edge + 2)
    is_pole = jnp.logical_and(i >= first_pole, i < first_pole + 2)
    east_i, west_i = lax.rem(i + 1, lon_count), lax.rem(i + lon_count - 1, lon_count)
    half = lon_count // 2

    def remote(src, dst, send, recv, lat, lon):
        return pltpu.make_async_remote_copy(
            src_ref=src, dst_ref=dst, send_sem=send, recv_sem=recv,
            device_id=(lat, lon), device_id_type=pl.DeviceIdType.MESH,
        )

    loads = [
        pltpu.make_async_copy(src, dst, loaded.at[k])
        for k, (src, dst) in enumerate(
            [
                (st_in, st_ref), (ce_in, ce_ref), (cn_in, cn_ref), (t1_in, t1_ref),
                (t2_in, t2_ref), (cut_in, cut_ref), (mask_in, mask_ref),
            ]
        )
    ]
    for load in loads:
        load.start()
    barrier = pltpu.get_barrier_semaphore()

    def greet(lat, lon):
        pl.semaphore_signal(
            barrier, inc=1, device_id=(lat, lon), device_id_type=pl.DeviceIdType.MESH
        )

    @pl.when(polar)
    def _():
        for step in range(1, lon_count):
            greet(a, lax.rem(i + step, lon_count))

        @pl.when(is_edge)
        def _():
            for lon in range(lon_count):
                greet(other, lon)

        @pl.when(jnp.logical_not(is_edge))
        def _():
            greet(other, i)

    @pl.when(jnp.logical_not(polar))
    def _():
        greet(a, east_i)
        greet(a, west_i)
        greet(3 - a, i)
        greet(other, first_edge)
        greet(other, first_edge + 1)

        @pl.when(jnp.logical_not(is_edge))
        def _():
            greet(other, i)

    for load in loads[:3]:
        load.wait()
    pad = jnp.zeros((wide - n_cols, n_rows, n_comp), jnp.float32)

    def rows_first(ref):
        return jnp.swapaxes(jnp.concatenate([ref[...], pad], axis=0), 0, 1)

    blocks[...] = rows_first(st_ref)
    cn_rows[...] = rows_first(cn_ref)
    to_east[2] = ce_ref[n_cols - 1]

    @pl.when(jnp.logical_not(polar))
    def _():
        to_east[0] = st_ref[n_cols - 2]
        to_east[1] = st_ref[n_cols - 1]
        to_west[0] = st_ref[0]
        to_west[1] = st_ref[1]

    @pl.when(polar)
    def _():
        lines[i] = blocks[i]

    @pl.when(a == 0)
    def _():
        cn_south[...] = jnp.zeros_like(cn_south)

    @pl.when(polar)
    def _():
        pl.semaphore_wait(barrier, lon_count - 1 + jnp.where(is_edge, lon_count, 1))

    @pl.when(jnp.logical_not(polar))
    def _():
        pl.semaphore_wait(barrier, 5 + jnp.where(is_edge, 0, 1))

    def row_copy(step):
        to = lax.rem(i + step, lon_count)
        return remote(blocks.at[to], lines.at[i], send_a.at[step], recv_a.at[step], a, to)

    cn_copy = remote(cn_rows.at[n_rows - 1], cn_south, send_cn, recv_cn, a + 1, i)
    edge_ce = remote(
        to_east.at[2], from_west.at[2], send_edge.at[0], recv_edge.at[0], a, east_i
    )
    edge_east = remote(to_east, from_west, send_edge.at[0], recv_edge.at[0], a, east_i)
    edge_west = remote(to_west, from_east, send_edge.at[1], recv_edge.at[1], a, west_i)
    raw_south = remote(
        blocks.at[pl.ds(0, 2)], ext.at[pl.ds(n_rows + 2, 2)],
        send_raw.at[0], recv_raw.at[1], a - 1, i,
    )
    raw_north = remote(
        blocks.at[pl.ds(n_rows - 2, 2)], ext.at[pl.ds(0, 2)],
        send_raw.at[1], recv_raw.at[0], a + 1, i,
    )

    @pl.when(polar)
    def _():
        for step in range(1, lon_count):
            row_copy(step).start()
        edge_ce.start()

    @pl.when(jnp.logical_not(polar))
    def _():
        edge_east.start()
        edge_west.start()
        raw_south.start()
        raw_north.start()

    @pl.when(a < lat_count - 1)
    def _():
        cn_copy.start()

    def line_copy(step):
        to = lax.rem(i + step, lon_count)
        return remote(
            synth.at[to], ext.at[i + 2], send_b.at[step], recv_rows.at[i + 2], a, to
        )

    pole_slot = jnp.where(southern, 1 - i, n_rows * 2 + 1 - i)
    edge_slot = jnp.where(southern, i - (n_rows - 2), n_rows + 2 + i)

    def pole_copy(step):
        to = lax.rem(i + step, lon_count)
        return remote(
            synth.at[lax.rem(to + half, lon_count)], ext.at[pole_slot],
            send_c.at[step], recv_rows.at[pole_slot], a, to,
        )

    def edge_copy(lon):
        return remote(
            synth.at[lon], ext.at[edge_slot], send_c.at[lon], recv_rows.at[edge_slot], other, lon
        )

    def slot_wait(slot):
        remote(blocks.at[0], ext.at[slot], send_b.at[0], recv_rows.at[slot], a, east_i).wait_recv()

    ce_rows[...] = rows_first(ce_ref)
    for load in loads[3:]:
        load.wait()

    @pl.when(polar)
    def _():
        lane = lax.broadcasted_iota(jnp.int32, (1, t1_ref.shape[1]), 1)
        wave = jnp.where(lane < n_waves, lane, lane - n_waves)
        kept = jnp.where(wave == 0, 1.0 / n_full, 2.0 / n_full).astype(jnp.float32)
        kept = jnp.where(wave <= cut_ref[i], kept, 0.0)
        weights = lax.dot_general(
            t1_ref[...] * kept, t2_ref[...], (((1,), (0,)), ((), ())), precision=HIGHEST,
            preferred_element_type=jnp.float32,
        )
        size = lon_count * wide
        dim = (lon_count, wide, 1)
        place = lax.broadcasted_iota(jnp.int32, dim, 1)
        at = lax.broadcasted_iota(jnp.int32, dim, 0) * n_cols
        at = at + jnp.where(place < n_cols + 2, place, place - wide)
        at = jnp.where(at < 0, at + n_full, jnp.where(at >= n_full, at - n_full, at))
        at = jnp.where((place >= n_cols + 2) & (place < wide - 2), -1, at).reshape(size, 1)
        lane = lax.broadcasted_iota(jnp.int32, (1, size), 1)
        start = jnp.zeros((1, size), jnp.int32)
        for q in range(1, lon_count):
            start = start + jnp.where(lane >= q * wide, 1, 0)
        inner = lane - start * wide
        source = jnp.where(inner < n_cols, start * n_cols + inner, -2)
        weights = jnp.where(mask_ref[i] == 1, weights, jnp.where(at == source, 1.0, 0.0))
        w_hi = weights.astype(jnp.bfloat16)
        w_lo = (weights - w_hi.astype(jnp.float32)).astype(jnp.bfloat16)
        for step in range(1, lon_count):
            row_copy(step).wait_recv()
        line = lines[...].reshape(size, n_comp)
        l_hi = line.astype(jnp.bfloat16)
        l_lo = (line - l_hi.astype(jnp.float32)).astype(jnp.bfloat16)

        def times(left, right):
            return lax.dot_general(
                left, right, (((1,), (0,)), ((), ())), preferred_element_type=jnp.float32
            )

        smooth = times(w_hi, l_hi) + (times(w_hi, l_lo) + times(w_lo, l_hi))
        synth[...] = smooth.reshape(lon_count, wide, n_comp)
        for step in range(1, lon_count):
            line_copy(step).start()

        @pl.when(is_edge)
        def _():
            for lon in range(lon_count):
                edge_copy(lon).start()

        @pl.when(is_pole)
        def _():
            for step in range(1, lon_count):
                pole_copy(step).start()
            ext[pole_slot] = synth[lax.rem(i + half, lon_count)]

        ext[i + 2] = synth[i]

    @pl.when(jnp.logical_not(polar))
    def _():
        edge_east.wait_recv()
        edge_west.wait_recv()
        place = lax.broadcasted_iota(jnp.int32, (wide, 1), 0)
        for r in range(n_rows):
            row = blocks[r]
            row = jnp.where(place == wide - 2, from_west[0, r : r + 1, :], row)
            row = jnp.where(place == wide - 1, from_west[1, r : r + 1, :], row)
            row = jnp.where(place == n_cols, from_east[0, r : r + 1, :], row)
            row = jnp.where(place == n_cols + 1, from_east[1, r : r + 1, :], row)
            ext[r + 2] = row

    @pl.when(polar)
    def _():
        edge_ce.wait_recv()

    @pl.when(a > 0)
    def _():
        cn_copy.wait_recv()

    @pl.when(southern)
    def _():
        raw_south.wait_recv()

    @pl.when(jnp.logical_not(southern))
    def _():
        raw_north.wait_recv()

    @pl.when(polar)
    def _():
        for step in range(1, lon_count):
            slot_wait(lax.rem(i + step, lon_count) + 2)
        for m in range(2):
            owner = first_pole + m
            slot = jnp.where(southern, 1 - m, n_rows + 3 - m)

            @pl.when(owner != i)
            def _():
                slot_wait(slot)

    @pl.when(jnp.logical_not(polar))
    def _():
        for m in range(2):
            slot_wait(jnp.where(southern, m, n_rows + 2 + m))

    def by_lat(values):
        chosen = jnp.float32(values[0])
        for lat in range(1, lat_count):
            chosen = jnp.where(a == lat, jnp.float32(values[lat]), chosen)
        return chosen

    def flux(far_lo, near_lo, near_hi, far_hi, courant):
        centred = (7.0 * (near_lo + near_hi) - (far_lo + far_hi)) * (1.0 / 12.0)
        return courant * centred - 0.5 * jnp.abs(courant) * (near_hi - near_lo)

    place = lax.broadcasted_iota(jnp.int32, (wide, 1), 0)
    below, advanced = None, []
    for f in range(-1, n_rows):
        faces = [lat * n_rows + f for lat in range(lat_count)]
        cos_face = by_lat([math.sin(min(g + 1, n_lat - 1 - g) * math.pi / n_lat) for g in faces])
        courant = cn_south[...] if f < 0 else cn_rows[f]
        stencil = [ext[f + 1 + t] for t in range(4)]
        weighted = cos_face * flux(*stencil, courant)
        if f >= 0:
            row = ext[f + 2]
            u = jnp.where(place == wide - 1, from_west[2, f : f + 1, :], ce_rows[f])
            east = flux(
                pltpu.roll(row, 1, 0), row, pltpu.roll(row, wide - 1, 0),
                pltpu.roll(row, wide - 2, 0), u,
            )
            zonal = -(east - pltpu.roll(east, 1, 0))
            per_cos = by_lat(
                [1.0 / math.sin((min(g, n_lat - 1 - g) + 0.5) * math.pi / n_lat) for g in faces]
            )
            advanced.append(row + zonal - (weighted - below) * per_cos)
        below = weighted
    out_ref[...] = jnp.swapaxes(jnp.stack(advanced), 0, 1)[:n_cols]

    @pl.when(polar)
    def _():
        for step in range(1, lon_count):
            row_copy(step).wait_send()
            line_copy(step).wait_send()
        edge_ce.wait_send()

        @pl.when(is_edge)
        def _():
            for lon in range(lon_count):
                edge_copy(lon).wait_send()

        @pl.when(is_pole)
        def _():
            for step in range(1, lon_count):
                pole_copy(step).wait_send()

    @pl.when(jnp.logical_not(polar))
    def _():
        edge_east.wait_send()
        edge_west.wait_send()
        raw_south.wait_send()
        raw_north.wait_send()

    @pl.when(a < lat_count - 1)
    def _():
        cn_copy.wait_send()


def local_fused(state, courant_east, courant_north, cutoff, filter_mask):
    n_rows, n_cols, n_comp = state.shape
    wide = spread(n_cols)
    synth, analyse, n_waves = wave_tables(n_cols, n_rows, n_rows * 4)
    flat = [
        jnp.transpose(x, (1, 0, 2))
        for x in (state, courant_east, courant_north)
    ]
    vmem = pl.BlockSpec(memory_space=pltpu.VMEM)
    block = pltpu.VMEM((n_rows, wide, n_comp), jnp.float32)
    dma = pltpu.SemaphoreType.DMA
    plane = pltpu.VMEM(flat[0].shape, jnp.float32)
    table = lambda value: pltpu.VMEM(value.shape, jnp.float32)
    edge = lambda count: pltpu.VMEM((count, n_rows, n_comp), jnp.float32)
    result = pl.pallas_call(
        functools.partial(fused_kernel, n_waves),
        out_shape=jax.ShapeDtypeStruct(flat[0].shape, jnp.float32),
        in_specs=[pl.BlockSpec(memory_space=pltpu.HBM)] * 7,
        out_specs=vmem,
        scratch_shapes=[
            pltpu.SMEM(cutoff.shape, jnp.int32), pltpu.SMEM(cutoff.shape, jnp.int32),
            plane, plane, plane, table(synth), table(analyse), dma((7,)),
            block, block, block,
            pltpu.VMEM((n_rows + 4, wide, n_comp), jnp.float32),
            block, block, edge(3), edge(2), edge(3), edge(2),
            pltpu.VMEM((wide, n_comp), jnp.float32),
            dma((n_rows,)), dma((n_rows,)), dma((n_rows,)), dma((n_rows + 4,)), dma((n_rows,)),
            dma((2,)), dma((2,)), dma, dma, dma((2,)), dma((2,)),
        ],
        compiler_params=pltpu.CompilerParams(
            collective_id=0, has_side_effects=True
        ),
    )(cutoff, filter_mask, *flat, synth, analyse)
    return jnp.transpose(result, (1, 0, 2))


def solution(mesh):
    placed = (
        P("lat", "lon", None),
        P("lat", "lon", None),
        P("lat", "lon", None),
        P("lat"),
        P("lat"),
    )

    def dispatch(*arrays):
        n_rows = arrays[0].shape[0]
        row_each = mesh.shape["lat"] == 4 and mesh.shape["lon"] == n_rows and n_rows >= 8
        return (local_fused if row_each else local)(*arrays)

    return jax.shard_map(
        dispatch, mesh=mesh, in_specs=placed, out_specs=P("lat", "lon", None), check_vma=False
    )
```

```python
import functools
import math

import jax
import jax.numpy as jnp
import numpy as np
from jax import lax
from jax.experimental import pallas as pl
from jax.experimental.pallas import tpu as pltpu
from jax.sharding import PartitionSpec as P

HIGHEST = lax.Precision.HIGHEST


def passed_along(block, axis, distance):
    devices = range(lax.axis_size(axis))
    route = [((i - distance) % len(devices), i) for i in devices]
    return lax.ppermute(block, axis, route)


def padded_2(value, sides, width):
    for axis, dim in sides:
        count, length = (lax.axis_size(axis), value.shape[dim])
        up = [(i, (i + 1) % count) for i in range(count)]
        down = [(j, i) for i, j in up]
        last = lax.slice_in_dim(value, length - width, length, axis=dim)
        initial = lax.slice_in_dim(value, 0, width, axis=dim)
        before = lax.ppermute(last, axis, up)
        after = lax.ppermute(initial, axis, down)
        value = jnp.concatenate([before, value, after], axis=dim)
    return value


def face_flux(far_lo, near_lo, near_hi, far_hi, courant):
    centred = (7.0 * (near_lo + near_hi) - (far_lo + far_hi)) / 12.0
    return courant * centred - 0.5 * jnp.abs(courant) * (near_hi - near_lo)


def build_table(n_full, n_half):
    points = jnp.arange(n_full, dtype=jnp.int32)
    waves = jnp.arange(n_half, dtype=jnp.int32)
    phase = points[:, None] * waves[None, :] % n_full
    angle = phase.astype(jnp.float32) * (2.0 * math.pi / n_full)
    return jnp.concatenate([jnp.cos(angle), jnp.sin(angle)], axis=1)


def pole_rows(field):
    return jnp.concatenate([field[:2][::-1], field[::-1][:2]], axis=0)


def send_rows(field):
    return lax.all_to_all(field, "lon", split_axis=2, concat_axis=1, tiled=True)


def return_rows(merged, lon_count):
    smooth = lax.all_to_all(merged, "lon", split_axis=1, concat_axis=2, tiled=True)
    partner = passed_along(pole_rows(smooth), "lon", lon_count // 2)
    return (smooth, partner)


def local(state, courant_east, courant_north, cutoff, filter_mask):
    n_rows, n_cols, n_comp = state.shape
    lon_count = lax.axis_size("lon")
    lat_count = lax.axis_size("lat")
    lat_index = lax.axis_index("lat")
    n_full = n_cols * lon_count
    n_half = n_full // 2 + 1
    n_lat = n_rows * lat_count
    fourier = build_table(n_full, n_half)
    waves = jnp.arange(n_half, dtype=jnp.int32)
    weights = jnp.where((waves == 0) | (waves == n_half - 1), 1.0 / n_full, 2.0 / n_full).astype(
        jnp.float32
    )
    row_lines = send_rows(state)
    kept = jnp.where(waves[None, :] <= cutoff[:, None], weights[None, :], 0.0)
    kept_both = jnp.concatenate([kept, kept], axis=1)
    coeffs = lax.dot_general(
        row_lines, fourier, (((1,), (0,)), ((), ())), precision=lax.Precision.HIGHEST
    )
    coeffs = coeffs * kept_both[:, None, :]
    synth = lax.dot_general(
        coeffs, fourier, (((2,), (1,)), ((), ())), precision=lax.Precision.HIGHEST
    )
    filtered = jnp.transpose(synth, (0, 2, 1))
    merged = jnp.where(filter_mask[:, None, None] == 1, filtered, row_lines)
    smooth, partner = return_rows(merged, lon_count)
    stacked = jnp.stack([smooth, courant_east, courant_north])
    padded = padded_2(stacked, (("lat", 1), ("lon", 2)), 2)
    zonal_p = padded[0, 2:-2]
    zonal_c = padded[1, 2:-2]
    east = face_flux(
        zonal_p[:, 0 : n_cols + 1],
        zonal_p[:, 1 : n_cols + 2],
        zonal_p[:, 2 : n_cols + 3],
        zonal_p[:, 3 : n_cols + 4],
        zonal_c[:, 1 : n_cols + 2],
    )
    zonal = -(east[:, 1:] - east[:, :-1])
    merid_p = padded[0, :, 2:-2]
    south = jnp.where(lat_index == 0, partner[:2], merid_p[:2])
    north = jnp.where(lat_index == lat_count - 1, partner[2:], merid_p[-2:])
    merid_p = jnp.concatenate([south, merid_p[2:-2], north], axis=0)
    merid_c = padded[2, :, 2:-2]
    north_flux = face_flux(
        merid_p[0 : n_rows + 1],
        merid_p[1 : n_rows + 2],
        merid_p[2 : n_rows + 3],
        merid_p[3 : n_rows + 4],
        merid_c[1 : n_rows + 2],
    )
    face_rows = lat_index * n_rows + jnp.arange(-1, n_rows, dtype=jnp.int32)
    cos_face = jnp.sin(
        jnp.minimum(face_rows + 1, n_lat - 1 - face_rows).astype(jnp.float32) * (math.pi / n_lat)
    )
    cell_rows = face_rows[1:]
    cos_cell = jnp.sin(
        (jnp.minimum(cell_rows, n_lat - 1 - cell_rows).astype(jnp.float32) + 0.5)
        * (math.pi / n_lat)
    )
    weighted = cos_face[:, None, None] * north_flux
    meridional = -(weighted[1:] - weighted[:-1]) / cos_cell[:, None, None]
    return smooth + zonal + meridional


def spread(n_cols):
    return -(-(n_cols + 4) // 8) * 8


def wave_tables(n_cols, lon_count, n_lat):
    n_full, wide = n_cols * lon_count, spread(n_cols)
    low = n_full // 8
    n_waves = low + (n_full // 2 - 1 - low) * (n_lat // 4 - 1) // (n_lat // 2) + 1
    lanes = -(-2 * n_waves // 128) * 128
    place = np.arange(wide)
    offset = np.where(place < n_cols + 2, place, place - wide)
    column = (np.arange(lon_count)[:, None] * n_cols + offset[None, :]).reshape(-1) % n_full
    angle = column[:, None] * np.arange(n_waves)[None, :] % n_full * (2.0 * np.pi / n_full)
    table = np.zeros((lon_count * wide, lanes), np.float64)
    table[:, : 2 * n_waves] = np.concatenate([np.cos(angle), np.sin(angle)], axis=1)
    given = np.tile((place < n_cols + 2) | (place >= wide - 2), lon_count)
    own = np.tile(place < n_cols, lon_count)
    synth = np.where(given[:, None], table, 0.0).astype(np.float32)
    analyse = np.where(own[:, None], table, 0.0).T.astype(np.float32)
    return synth, analyse, n_waves


def fused_kernel(
    n_waves, cut_in, mask_in, st_in, ce_in, cn_in, t1_in, t2_in, out_ref,
    cut_ref, mask_ref, st_ref, ce_ref, cn_ref, t1_ref, t2_ref, loaded,
    blocks, lines, synth, ext, ce_rows, cn_rows, to_east, to_west, from_west, from_east, cn_south,
    send_a, recv_a, send_b, recv_rows, send_c, send_raw, recv_raw, send_cn, recv_cn,
    send_edge, recv_edge,
):
    n_rows, wide, n_comp = blocks.shape
    n_cols = st_ref.shape[0]
    n_full = n_rows * n_cols
    lat_count, lon_count = lax.axis_size("lat"), n_rows
    n_lat = n_rows * lat_count
    a, i = lax.axis_index("lat"), lax.axis_index("lon")
    southern = a < 2
    polar = jnp.logical_or(a == 0, a == lat_count - 1)
    other = jnp.where(southern, 1 - a, 5 - a)
    first_edge = jnp.where(southern, n_rows - 2, 0)
    first_pole = jnp.where(southern, 0, n_rows - 2)
    is_edge = jnp.logical_and(i >= first_edge, i < first_edge + 2)
    is_pole = jnp.logical_and(i >= first_pole, i < first_pole + 2)
    east_i, west_i = lax.rem(i + 1, lon_count), lax.rem(i + lon_count - 1, lon_count)
    half = lon_count // 2

    def remote(src, dst, send, recv, lat, lon):
        return pltpu.make_async_remote_copy(
            src_ref=src, dst_ref=dst, send_sem=send, recv_sem=recv,
            device_id=(lat, lon), device_id_type=pl.DeviceIdType.MESH,
        )

    loads = [
        pltpu.make_async_copy(src, dst, loaded.at[k])
        for k, (src, dst) in enumerate(
            [
                (st_in, st_ref), (ce_in, ce_ref), (cn_in, cn_ref), (t1_in, t1_ref),
                (t2_in, t2_ref), (cut_in, cut_ref), (mask_in, mask_ref),
            ]
        )
    ]
    for load in loads:
        load.start()
    barrier = pltpu.get_barrier_semaphore()

    def greet(lat, lon):
        pl.semaphore_signal(
            barrier, inc=1, device_id=(lat, lon), device_id_type=pl.DeviceIdType.MESH
        )

    @pl.when(polar)
    def _():
        for step in range(1, lon_count):
            greet(a, lax.rem(i + step, lon_count))

        @pl.when(is_edge)
        def _():
            for lon in range(lon_count):
                greet(other, lon)

        @pl.when(jnp.logical_not(is_edge))
        def _():
            greet(other, i)

    @pl.when(jnp.logical_not(polar))
    def _():
        greet(a, east_i)
        greet(a, west_i)
        greet(3 - a, i)
        greet(other, first_edge)
        greet(other, first_edge + 1)

        @pl.when(jnp.logical_not(is_edge))
        def _():
            greet(other, i)

    loads[0].wait()
    pad = jnp.zeros((wide - n_cols, n_rows, n_comp), jnp.float32)

    def rows_first(ref):
        return jnp.swapaxes(jnp.concatenate([ref[...], pad], axis=0), 0, 1)

    blocks[...] = rows_first(st_ref)

    @pl.when(jnp.logical_not(polar))
    def _():
        to_east[0] = st_ref[n_cols - 2]
        to_east[1] = st_ref[n_cols - 1]
        to_west[0] = st_ref[0]
        to_west[1] = st_ref[1]

    @pl.when(polar)
    def _():
        lines[i] = blocks[i]

    @pl.when(a == 0)
    def _():
        cn_south[...] = jnp.zeros_like(cn_south)

    @pl.when(polar)
    def _():
        pl.semaphore_wait(barrier, lon_count - 1 + jnp.where(is_edge, lon_count, 1))

    @pl.when(jnp.logical_not(polar))
    def _():
        pl.semaphore_wait(barrier, 5 + jnp.where(is_edge, 0, 1))

    order = sorted(range(1, lon_count), key=lambda step: abs(step - half))

    def row_copy(step):
        to = lax.rem(i + step, lon_count)
        return remote(blocks.at[to], lines.at[i], send_a.at[step], recv_a.at[step], a, to)

    cn_copy = remote(cn_rows.at[n_rows - 1], cn_south, send_cn, recv_cn, a + 1, i)
    edge_ce = remote(
        to_east.at[2], from_west.at[2], send_edge.at[0], recv_edge.at[0], a, east_i
    )
    edge_east = remote(to_east, from_west, send_edge.at[0], recv_edge.at[0], a, east_i)
    edge_west = remote(to_west, from_east, send_edge.at[1], recv_edge.at[1], a, west_i)
    raw_south = remote(
        blocks.at[pl.ds(0, 2)], ext.at[pl.ds(n_rows + 2, 2)],
        send_raw.at[0], recv_raw.at[1], a - 1, i,
    )
    raw_north = remote(
        blocks.at[pl.ds(n_rows - 2, 2)], ext.at[pl.ds(0, 2)],
        send_raw.at[1], recv_raw.at[0], a + 1, i,
    )

    @pl.when(polar)
    def _():
        for step in order:
            row_copy(step).start()

    @pl.when(jnp.logical_not(polar))
    def _():
        edge_west.start()
        raw_south.start()
        raw_north.start()

    for load in loads[1:3]:
        load.wait()
    to_east[2] = ce_ref[n_cols - 1]
    cn_rows[...] = rows_first(cn_ref)

    @pl.when(polar)
    def _():
        edge_ce.start()

    @pl.when(jnp.logical_not(polar))
    def _():
        edge_east.start()

    @pl.when(a < lat_count - 1)
    def _():
        cn_copy.start()

    def line_copy(step):
        to = lax.rem(i + step, lon_count)
        return remote(
            synth.at[to], ext.at[i + 2], send_b.at[step], recv_rows.at[i + 2], a, to
        )

    pole_slot = jnp.where(southern, 1 - i, n_rows * 2 + 1 - i)
    edge_slot = jnp.where(southern, i - (n_rows - 2), n_rows + 2 + i)

    def pole_copy(step):
        to = lax.rem(i + step, lon_count)
        return remote(
            synth.at[lax.rem(to + half, lon_count)], ext.at[pole_slot],
            send_c.at[step], recv_rows.at[pole_slot], a, to,
        )

    def edge_copy(step):
        to = lax.rem(i + step, lon_count)
        return remote(
            synth.at[to], ext.at[edge_slot], send_c.at[step], recv_rows.at[edge_slot], other, to
        )

    def slot_wait(slot):
        remote(blocks.at[0], ext.at[slot], send_b.at[0], recv_rows.at[slot], a, east_i).wait_recv()

    ce_rows[...] = rows_first(ce_ref)
    for load in loads[3:]:
        load.wait()

    @pl.when(polar)
    def _():
        lane = lax.broadcasted_iota(jnp.int32, (1, t1_ref.shape[1]), 1)
        wave = jnp.where(lane < n_waves, lane, lane - n_waves)
        kept = jnp.where(wave == 0, 1.0 / n_full, 2.0 / n_full).astype(jnp.float32)
        kept = jnp.where(wave <= cut_ref[i], kept, 0.0)
        weights = lax.dot_general(
            t1_ref[...] * kept, t2_ref[...], (((1,), (0,)), ((), ())), precision=HIGHEST,
            preferred_element_type=jnp.float32,
        )
        size = lon_count * wide
        dim = (lon_count, wide, 1)
        place = lax.broadcasted_iota(jnp.int32, dim, 1)
        at = lax.broadcasted_iota(jnp.int32, dim, 0) * n_cols
        at = at + jnp.where(place < n_cols + 2, place, place - wide)
        at = jnp.where(at < 0, at + n_full, jnp.where(at >= n_full, at - n_full, at))
        at = jnp.where((place >= n_cols + 2) & (place < wide - 2), -1, at).reshape(size, 1)
        lane = lax.broadcasted_iota(jnp.int32, (1, size), 1)
        start = jnp.zeros((1, size), jnp.int32)
        for q in range(1, lon_count):
            start = start + jnp.where(lane >= q * wide, 1, 0)
        inner = lane - start * wide
        source = jnp.where(inner < n_cols, start * n_cols + inner, -2)
        weights = jnp.where(mask_ref[i] == 1, weights, jnp.where(at == source, 1.0, 0.0))
        w_hi = weights.astype(jnp.bfloat16)
        w_lo = (weights - w_hi.astype(jnp.float32)).astype(jnp.bfloat16)
        for step in range(1, lon_count):
            row_copy(step).wait_recv()
        line = lines[...].reshape(size, n_comp)
        l_hi = line.astype(jnp.bfloat16)
        l_lo = (line - l_hi.astype(jnp.float32)).astype(jnp.bfloat16)

        def times(left, right):
            return lax.dot_general(
                left, right, (((1,), (0,)), ((), ())), preferred_element_type=jnp.float32
            )

        smooth = times(w_hi, l_hi) + (times(w_hi, l_lo) + times(w_lo, l_hi))
        synth[...] = smooth.reshape(lon_count, wide, n_comp)

        @pl.when(is_edge)
        def _():
            for step in order:
                line_copy(step).start()
                edge_copy(step).start()
            edge_copy(0).start()

        @pl.when(is_pole)
        def _():
            for step in order:
                line_copy(step).start()
                pole_copy(step).start()
            ext[pole_slot] = synth[lax.rem(i + half, lon_count)]

        @pl.when(jnp.logical_not(jnp.logical_or(is_edge, is_pole)))
        def _():
            for step in order:
                line_copy(step).start()

        ext[i + 2] = synth[i]

    @pl.when(jnp.logical_not(polar))
    def _():
        edge_east.wait_recv()
        edge_west.wait_recv()
        place = lax.broadcasted_iota(jnp.int32, (wide, 1), 0)
        for r in range(n_rows):
            row = blocks[r]
            row = jnp.where(place == wide - 2, from_west[0, r : r + 1, :], row)
            row = jnp.where(place == wide - 1, from_west[1, r : r + 1, :], row)
            row = jnp.where(place == n_cols, from_east[0, r : r + 1, :], row)
            row = jnp.where(place == n_cols + 1, from_east[1, r : r + 1, :], row)
            ext[r + 2] = row

    @pl.when(polar)
    def _():
        edge_ce.wait_recv()

    @pl.when(a > 0)
    def _():
        cn_copy.wait_recv()

    @pl.when(southern)
    def _():
        raw_south.wait_recv()

    @pl.when(jnp.logical_not(southern))
    def _():
        raw_north.wait_recv()

    @pl.when(polar)
    def _():
        for step in range(1, lon_count):
            slot_wait(lax.rem(i + step, lon_count) + 2)
        for m in range(2):
            owner = first_pole + m
            slot = jnp.where(southern, 1 - m, n_rows + 3 - m)

            @pl.when(owner != i)
            def _():
                slot_wait(slot)

    @pl.when(jnp.logical_not(polar))
    def _():
        for m in range(2):
            slot_wait(jnp.where(southern, m, n_rows + 2 + m))

    def by_lat(values):
        chosen = jnp.float32(values[0])
        for lat in range(1, lat_count):
            chosen = jnp.where(a == lat, jnp.float32(values[lat]), chosen)
        return chosen

    def flux(far_lo, near_lo, near_hi, far_hi, courant):
        centred = (7.0 * (near_lo + near_hi) - (far_lo + far_hi)) * (1.0 / 12.0)
        return courant * centred - 0.5 * jnp.abs(courant) * (near_hi - near_lo)

    place = lax.broadcasted_iota(jnp.int32, (wide, 1), 0)
    below = None
    for f in range(-1, n_rows):
        faces = [lat * n_rows + f for lat in range(lat_count)]
        cos_face = by_lat([math.sin(min(g + 1, n_lat - 1 - g) * math.pi / n_lat) for g in faces])
        courant = cn_south[...] if f < 0 else cn_rows[f]
        stencil = [ext[f + 1 + t] for t in range(4)]
        weighted = cos_face * flux(*stencil, courant)
        if f >= 0:
            row = ext[f + 2]
            u = jnp.where(place == wide - 1, from_west[2, f : f + 1, :], ce_rows[f])
            east = flux(
                pltpu.roll(row, 1, 0), row, pltpu.roll(row, wide - 1, 0),
                pltpu.roll(row, wide - 2, 0), u,
            )
            zonal = -(east - pltpu.roll(east, 1, 0))
            per_cos = by_lat(
                [1.0 / math.sin((min(g, n_lat - 1 - g) + 0.5) * math.pi / n_lat) for g in faces]
            )
            out_ref[f] = (row + zonal - (weighted - below) * per_cos)[:n_cols]
        below = weighted

    @pl.when(polar)
    def _():
        for step in range(1, lon_count):
            row_copy(step).wait_send()
            line_copy(step).wait_send()
        edge_ce.wait_send()

        @pl.when(is_edge)
        def _():
            for step in range(lon_count):
                edge_copy(step).wait_send()

        @pl.when(is_pole)
        def _():
            for step in range(1, lon_count):
                pole_copy(step).wait_send()

    @pl.when(jnp.logical_not(polar))
    def _():
        edge_east.wait_send()
        edge_west.wait_send()
        raw_south.wait_send()
        raw_north.wait_send()

    @pl.when(a < lat_count - 1)
    def _():
        cn_copy.wait_send()


def local_fused(state, courant_east, courant_north, cutoff, filter_mask):
    n_rows, n_cols, n_comp = state.shape
    wide = spread(n_cols)
    synth, analyse, n_waves = wave_tables(n_cols, n_rows, n_rows * 4)
    flat = [
        jnp.transpose(x, (1, 0, 2))
        for x in (state, courant_east, courant_north)
    ]
    vmem = pl.BlockSpec(memory_space=pltpu.VMEM)
    block = pltpu.VMEM((n_rows, wide, n_comp), jnp.float32)
    dma = pltpu.SemaphoreType.DMA
    plane = pltpu.VMEM(flat[0].shape, jnp.float32)
    table = lambda value: pltpu.VMEM(value.shape, jnp.float32)
    edge = lambda count: pltpu.VMEM((count, n_rows, n_comp), jnp.float32)
    return pl.pallas_call(
        functools.partial(fused_kernel, n_waves),
        out_shape=jax.ShapeDtypeStruct(state.shape, jnp.float32),
        in_specs=[pl.BlockSpec(memory_space=pltpu.HBM)] * 7,
        out_specs=vmem,
        scratch_shapes=[
            pltpu.SMEM(cutoff.shape, jnp.int32), pltpu.SMEM(cutoff.shape, jnp.int32),
            plane, plane, plane, table(synth), table(analyse), dma((7,)),
            block, block, block,
            pltpu.VMEM((n_rows + 4, wide, n_comp), jnp.float32),
            block, block, edge(3), edge(2), edge(3), edge(2),
            pltpu.VMEM((wide, n_comp), jnp.float32),
            dma((n_rows,)), dma((n_rows,)), dma((n_rows,)), dma((n_rows + 4,)), dma((n_rows,)),
            dma((2,)), dma((2,)), dma, dma, dma((2,)), dma((2,)),
        ],
        compiler_params=pltpu.CompilerParams(
            collective_id=0, has_side_effects=True
        ),
    )(cutoff, filter_mask, *flat, synth, analyse)


def solution(mesh):
    placed = (
        P("lat", "lon", None),
        P("lat", "lon", None),
        P("lat", "lon", None),
        P("lat"),
        P("lat"),
    )

    def dispatch(*arrays):
        n_rows = arrays[0].shape[0]
        row_each = mesh.shape["lat"] == 4 and mesh.shape["lon"] == n_rows and n_rows >= 8
        return (local_fused if row_each else local)(*arrays)

    return jax.shard_map(
        dispatch, mesh=mesh, in_specs=placed, out_specs=P("lat", "lon", None), check_vma=False
    )
```

```python
import functools
import math

import jax
import jax.numpy as jnp
import numpy as np
from jax import lax
from jax.experimental import pallas as pl
from jax.experimental.pallas import tpu as pltpu
from jax.sharding import PartitionSpec as P

HIGHEST = lax.Precision.HIGHEST


def passed_along(block, axis, distance):
    devices = range(lax.axis_size(axis))
    route = [((i - distance) % len(devices), i) for i in devices]
    return lax.ppermute(block, axis, route)


def padded_2(value, sides, width):
    for axis, dim in sides:
        count, length = (lax.axis_size(axis), value.shape[dim])
        up = [(i, (i + 1) % count) for i in range(count)]
        down = [(j, i) for i, j in up]
        last = lax.slice_in_dim(value, length - width, length, axis=dim)
        initial = lax.slice_in_dim(value, 0, width, axis=dim)
        before = lax.ppermute(last, axis, up)
        after = lax.ppermute(initial, axis, down)
        value = jnp.concatenate([before, value, after], axis=dim)
    return value


def face_flux(far_lo, near_lo, near_hi, far_hi, courant):
    centred = (7.0 * (near_lo + near_hi) - (far_lo + far_hi)) / 12.0
    return courant * centred - 0.5 * jnp.abs(courant) * (near_hi - near_lo)


def build_table(n_full, n_half):
    points = jnp.arange(n_full, dtype=jnp.int32)
    waves = jnp.arange(n_half, dtype=jnp.int32)
    phase = points[:, None] * waves[None, :] % n_full
    angle = phase.astype(jnp.float32) * (2.0 * math.pi / n_full)
    return jnp.concatenate([jnp.cos(angle), jnp.sin(angle)], axis=1)


def pole_rows(field):
    return jnp.concatenate([field[:2][::-1], field[::-1][:2]], axis=0)


def send_rows(field):
    return lax.all_to_all(field, "lon", split_axis=2, concat_axis=1, tiled=True)


def return_rows(merged, lon_count):
    smooth = lax.all_to_all(merged, "lon", split_axis=1, concat_axis=2, tiled=True)
    partner = passed_along(pole_rows(smooth), "lon", lon_count // 2)
    return (smooth, partner)


def local(state, courant_east, courant_north, cutoff, filter_mask):
    n_rows, n_cols, n_comp = state.shape
    lon_count = lax.axis_size("lon")
    lat_count = lax.axis_size("lat")
    lat_index = lax.axis_index("lat")
    n_full = n_cols * lon_count
    n_half = n_full // 2 + 1
    n_lat = n_rows * lat_count
    fourier = build_table(n_full, n_half)
    waves = jnp.arange(n_half, dtype=jnp.int32)
    weights = jnp.where((waves == 0) | (waves == n_half - 1), 1.0 / n_full, 2.0 / n_full).astype(
        jnp.float32
    )
    row_lines = send_rows(state)
    kept = jnp.where(waves[None, :] <= cutoff[:, None], weights[None, :], 0.0)
    kept_both = jnp.concatenate([kept, kept], axis=1)
    coeffs = lax.dot_general(
        row_lines, fourier, (((1,), (0,)), ((), ())), precision=lax.Precision.HIGHEST
    )
    coeffs = coeffs * kept_both[:, None, :]
    synth = lax.dot_general(
        coeffs, fourier, (((2,), (1,)), ((), ())), precision=lax.Precision.HIGHEST
    )
    filtered = jnp.transpose(synth, (0, 2, 1))
    merged = jnp.where(filter_mask[:, None, None] == 1, filtered, row_lines)
    smooth, partner = return_rows(merged, lon_count)
    stacked = jnp.stack([smooth, courant_east, courant_north])
    padded = padded_2(stacked, (("lat", 1), ("lon", 2)), 2)
    zonal_p = padded[0, 2:-2]
    zonal_c = padded[1, 2:-2]
    east = face_flux(
        zonal_p[:, 0 : n_cols + 1],
        zonal_p[:, 1 : n_cols + 2],
        zonal_p[:, 2 : n_cols + 3],
        zonal_p[:, 3 : n_cols + 4],
        zonal_c[:, 1 : n_cols + 2],
    )
    zonal = -(east[:, 1:] - east[:, :-1])
    merid_p = padded[0, :, 2:-2]
    south = jnp.where(lat_index == 0, partner[:2], merid_p[:2])
    north = jnp.where(lat_index == lat_count - 1, partner[2:], merid_p[-2:])
    merid_p = jnp.concatenate([south, merid_p[2:-2], north], axis=0)
    merid_c = padded[2, :, 2:-2]
    north_flux = face_flux(
        merid_p[0 : n_rows + 1],
        merid_p[1 : n_rows + 2],
        merid_p[2 : n_rows + 3],
        merid_p[3 : n_rows + 4],
        merid_c[1 : n_rows + 2],
    )
    face_rows = lat_index * n_rows + jnp.arange(-1, n_rows, dtype=jnp.int32)
    cos_face = jnp.sin(
        jnp.minimum(face_rows + 1, n_lat - 1 - face_rows).astype(jnp.float32) * (math.pi / n_lat)
    )
    cell_rows = face_rows[1:]
    cos_cell = jnp.sin(
        (jnp.minimum(cell_rows, n_lat - 1 - cell_rows).astype(jnp.float32) + 0.5)
        * (math.pi / n_lat)
    )
    weighted = cos_face[:, None, None] * north_flux
    meridional = -(weighted[1:] - weighted[:-1]) / cos_cell[:, None, None]
    return smooth + zonal + meridional


def spread(n_cols):
    return -(-(n_cols + 4) // 8) * 8


def wave_tables(n_cols, lon_count, n_lat):
    n_full, wide = n_cols * lon_count, spread(n_cols)
    low = n_full // 8
    n_waves = low + (n_full // 2 - 1 - low) * (n_lat // 4 - 1) // (n_lat // 2) + 1
    lanes = -(-2 * n_waves // 128) * 128
    place = np.arange(wide)
    offset = np.where(place < n_cols + 2, place, place - wide)
    column = (np.arange(lon_count)[:, None] * n_cols + offset[None, :]).reshape(-1) % n_full
    angle = column[:, None] * np.arange(n_waves)[None, :] % n_full * (2.0 * np.pi / n_full)
    table = np.zeros((lon_count * wide, lanes), np.float64)
    table[:, : 2 * n_waves] = np.concatenate([np.cos(angle), np.sin(angle)], axis=1)
    given = np.tile((place < n_cols + 2) | (place >= wide - 2), lon_count)
    own = np.tile(place < n_cols, lon_count)
    synth = np.where(given[:, None], table, 0.0).astype(np.float32)
    analyse = np.where(own[:, None], table, 0.0).T.astype(np.float32)
    return synth, analyse, n_waves


def fused_kernel(
    n_waves, cut_in, mask_in, st_in, ce_in, cn_in, t1_in, t2_in, out_ref,
    cut_ref, mask_ref, st_ref, ce_ref, cn_ref, t1_ref, t2_ref, loaded,
    blocks, lines, synth, ext, ce_rows, cn_rows, to_east, to_west, from_west, from_east, cn_south,
    send_a, recv_a, send_b, recv_rows, send_c, send_raw, recv_raw, send_cn, recv_cn,
    send_edge, recv_edge,
):
    n_rows, wide, n_comp = blocks.shape
    n_cols = st_ref.shape[0]
    n_full = n_rows * n_cols
    lat_count, lon_count = lax.axis_size("lat"), n_rows
    n_lat = n_rows * lat_count
    a, i = lax.axis_index("lat"), lax.axis_index("lon")
    southern = a < 2
    polar = jnp.logical_or(a == 0, a == lat_count - 1)
    other = jnp.where(southern, 1 - a, 5 - a)
    first_edge = jnp.where(southern, n_rows - 2, 0)
    first_pole = jnp.where(southern, 0, n_rows - 2)
    is_edge = jnp.logical_and(i >= first_edge, i < first_edge + 2)
    is_pole = jnp.logical_and(i >= first_pole, i < first_pole + 2)
    east_i, west_i = lax.rem(i + 1, lon_count), lax.rem(i + lon_count - 1, lon_count)
    half = lon_count // 2

    def remote(src, dst, send, recv, lat, lon):
        return pltpu.make_async_remote_copy(
            src_ref=src, dst_ref=dst, send_sem=send, recv_sem=recv,
            device_id=(lat, lon), device_id_type=pl.DeviceIdType.MESH,
        )

    loads = [
        pltpu.make_async_copy(src, dst, loaded.at[k])
        for k, (src, dst) in enumerate(
            [
                (st_in, st_ref), (ce_in, ce_ref), (cn_in, cn_ref), (t1_in, t1_ref),
                (t2_in, t2_ref), (cut_in, cut_ref), (mask_in, mask_ref),
            ]
        )
    ]
    for load in loads:
        load.start()
    barrier = pltpu.get_barrier_semaphore()

    def greet(lat, lon):
        pl.semaphore_signal(
            barrier, inc=1, device_id=(lat, lon), device_id_type=pl.DeviceIdType.MESH
        )

    @pl.when(polar)
    def _():
        for step in range(1, lon_count):
            greet(a, lax.rem(i + step, lon_count))

        @pl.when(is_edge)
        def _():
            for lon in range(lon_count):
                greet(other, lon)

        @pl.when(jnp.logical_not(is_edge))
        def _():
            greet(other, i)

    @pl.when(jnp.logical_not(polar))
    def _():
        greet(a, east_i)
        greet(a, west_i)
        greet(3 - a, i)
        greet(other, first_edge)
        greet(other, first_edge + 1)

        @pl.when(jnp.logical_not(is_edge))
        def _():
            greet(other, i)

    loads[0].wait()
    pad = jnp.zeros((wide - n_cols, n_rows, n_comp), jnp.float32)

    def rows_first(ref):
        return jnp.swapaxes(jnp.concatenate([ref[...], pad], axis=0), 0, 1)

    blocks[...] = rows_first(st_ref)

    @pl.when(jnp.logical_not(polar))
    def _():
        to_east[0] = st_ref[n_cols - 2]
        to_east[1] = st_ref[n_cols - 1]
        to_west[0] = st_ref[0]
        to_west[1] = st_ref[1]

    @pl.when(polar)
    def _():
        lines[i] = blocks[i]

    @pl.when(a == 0)
    def _():
        cn_south[...] = jnp.zeros_like(cn_south)

    @pl.when(polar)
    def _():
        pl.semaphore_wait(barrier, lon_count - 1 + jnp.where(is_edge, lon_count, 1))

    @pl.when(jnp.logical_not(polar))
    def _():
        pl.semaphore_wait(barrier, 5 + jnp.where(is_edge, 0, 1))

    order = sorted(range(1, lon_count), key=lambda step: -abs(step - half))

    def row_copy(step):
        to = lax.rem(i + step, lon_count)
        return remote(blocks.at[to], lines.at[i], send_a.at[step], recv_a.at[step], a, to)

    cn_copy = remote(cn_rows.at[n_rows - 1], cn_south, send_cn, recv_cn, a + 1, i)
    edge_ce = remote(
        to_east.at[2], from_west.at[2], send_edge.at[0], recv_edge.at[0], a, east_i
    )
    edge_east = remote(to_east, from_west, send_edge.at[0], recv_edge.at[0], a, east_i)
    edge_west = remote(to_west, from_east, send_edge.at[1], recv_edge.at[1], a, west_i)
    raw_south = remote(
        blocks.at[pl.ds(0, 2)], ext.at[pl.ds(n_rows + 2, 2)],
        send_raw.at[0], recv_raw.at[1], a - 1, i,
    )
    raw_north = remote(
        blocks.at[pl.ds(n_rows - 2, 2)], ext.at[pl.ds(0, 2)],
        send_raw.at[1], recv_raw.at[0], a + 1, i,
    )

    @pl.when(polar)
    def _():
        for step in order:
            row_copy(step).start()

    @pl.when(jnp.logical_not(polar))
    def _():
        edge_west.start()
        raw_south.start()
        raw_north.start()

    for load in loads[1:3]:
        load.wait()
    to_east[2] = ce_ref[n_cols - 1]
    cn_rows[...] = rows_first(cn_ref)

    @pl.when(polar)
    def _():
        edge_ce.start()

    @pl.when(jnp.logical_not(polar))
    def _():
        edge_east.start()

    @pl.when(a < lat_count - 1)
    def _():
        cn_copy.start()

    def line_copy(step):
        to = lax.rem(i + step, lon_count)
        return remote(
            synth.at[to], ext.at[i + 2], send_b.at[step], recv_rows.at[i + 2], a, to
        )

    pole_slot = jnp.where(southern, 1 - i, n_rows * 2 + 1 - i)
    edge_slot = jnp.where(southern, i - (n_rows - 2), n_rows + 2 + i)

    def pole_copy(step):
        to = lax.rem(i + step, lon_count)
        return remote(
            synth.at[lax.rem(to + half, lon_count)], ext.at[pole_slot],
            send_c.at[step], recv_rows.at[pole_slot], a, to,
        )

    def edge_copy(lon):
        return remote(
            synth.at[lon], ext.at[edge_slot], send_c.at[lon], recv_rows.at[edge_slot], other, lon
        )

    def slot_wait(slot):
        remote(blocks.at[0], ext.at[slot], send_b.at[0], recv_rows.at[slot], a, east_i).wait_recv()

    ce_rows[...] = rows_first(ce_ref)
    for load in loads[3:]:
        load.wait()

    @pl.when(polar)
    def _():
        lane = lax.broadcasted_iota(jnp.int32, (1, t1_ref.shape[1]), 1)
        wave = jnp.where(lane < n_waves, lane, lane - n_waves)
        kept = jnp.where(wave == 0, 1.0 / n_full, 2.0 / n_full).astype(jnp.float32)
        kept = jnp.where(wave <= cut_ref[i], kept, 0.0)
        weights = lax.dot_general(
            t1_ref[...] * kept, t2_ref[...], (((1,), (0,)), ((), ())), precision=HIGHEST,
            preferred_element_type=jnp.float32,
        )
        size = lon_count * wide
        dim = (lon_count, wide, 1)
        place = lax.broadcasted_iota(jnp.int32, dim, 1)
        at = lax.broadcasted_iota(jnp.int32, dim, 0) * n_cols
        at = at + jnp.where(place < n_cols + 2, place, place - wide)
        at = jnp.where(at < 0, at + n_full, jnp.where(at >= n_full, at - n_full, at))
        at = jnp.where((place >= n_cols + 2) & (place < wide - 2), -1, at).reshape(size, 1)
        lane = lax.broadcasted_iota(jnp.int32, (1, size), 1)
        start = jnp.zeros((1, size), jnp.int32)
        for q in range(1, lon_count):
            start = start + jnp.where(lane >= q * wide, 1, 0)
        inner = lane - start * wide
        source = jnp.where(inner < n_cols, start * n_cols + inner, -2)
        weights = jnp.where(mask_ref[i] == 1, weights, jnp.where(at == source, 1.0, 0.0))
        w_hi = weights.astype(jnp.bfloat16)
        w_lo = (weights - w_hi.astype(jnp.float32)).astype(jnp.bfloat16)
        for step in range(1, lon_count):
            row_copy(step).wait_recv()
        line = lines[...].reshape(size, n_comp)
        l_hi = line.astype(jnp.bfloat16)
        l_lo = (line - l_hi.astype(jnp.float32)).astype(jnp.bfloat16)

        def times(left, right):
            return lax.dot_general(
                left, right, (((1,), (0,)), ((), ())), preferred_element_type=jnp.float32
            )

        smooth = times(w_hi, l_hi) + (times(w_hi, l_lo) + times(w_lo, l_hi))
        synth[...] = smooth.reshape(lon_count, wide, n_comp)
        for step in range(1, lon_count):
            line_copy(step).start()

        @pl.when(is_edge)
        def _():
            for lon in range(lon_count):
                edge_copy(lon).start()

        @pl.when(is_pole)
        def _():
            for step in range(1, lon_count):
                pole_copy(step).start()
            ext[pole_slot] = synth[lax.rem(i + half, lon_count)]

        ext[i + 2] = synth[i]

    @pl.when(jnp.logical_not(polar))
    def _():
        edge_east.wait_recv()
        edge_west.wait_recv()
        place = lax.broadcasted_iota(jnp.int32, (wide, 1), 0)
        for r in range(n_rows):
            row = blocks[r]
            row = jnp.where(place == wide - 2, from_west[0, r : r + 1, :], row)
            row = jnp.where(place == wide - 1, from_west[1, r : r + 1, :], row)
            row = jnp.where(place == n_cols, from_east[0, r : r + 1, :], row)
            row = jnp.where(place == n_cols + 1, from_east[1, r : r + 1, :], row)
            ext[r + 2] = row

    @pl.when(polar)
    def _():
        edge_ce.wait_recv()

    @pl.when(a > 0)
    def _():
        cn_copy.wait_recv()

    @pl.when(southern)
    def _():
        raw_south.wait_recv()

    @pl.when(jnp.logical_not(southern))
    def _():
        raw_north.wait_recv()

    @pl.when(polar)
    def _():
        for step in range(1, lon_count):
            slot_wait(lax.rem(i + step, lon_count) + 2)
        for m in range(2):
            owner = first_pole + m
            slot = jnp.where(southern, 1 - m, n_rows + 3 - m)

            @pl.when(owner != i)
            def _():
                slot_wait(slot)

    @pl.when(jnp.logical_not(polar))
    def _():
        for m in range(2):
            slot_wait(jnp.where(southern, m, n_rows + 2 + m))

    def by_lat(values):
        chosen = jnp.float32(values[0])
        for lat in range(1, lat_count):
            chosen = jnp.where(a == lat, jnp.float32(values[lat]), chosen)
        return chosen

    def flux(far_lo, near_lo, near_hi, far_hi, courant):
        centred = (7.0 * (near_lo + near_hi) - (far_lo + far_hi)) * (1.0 / 12.0)
        return courant * centred - 0.5 * jnp.abs(courant) * (near_hi - near_lo)

    place = lax.broadcasted_iota(jnp.int32, (wide, 1), 0)
    below, advanced = None, []
    for f in range(-1, n_rows):
        faces = [lat * n_rows + f for lat in range(lat_count)]
        cos_face = by_lat([math.sin(min(g + 1, n_lat - 1 - g) * math.pi / n_lat) for g in faces])
        courant = cn_south[...] if f < 0 else cn_rows[f]
        stencil = [ext[f + 1 + t] for t in range(4)]
        weighted = cos_face * flux(*stencil, courant)
        if f >= 0:
            row = ext[f + 2]
            u = jnp.where(place == wide - 1, from_west[2, f : f + 1, :], ce_rows[f])
            east = flux(
                pltpu.roll(row, 1, 0), row, pltpu.roll(row, wide - 1, 0),
                pltpu.roll(row, wide - 2, 0), u,
            )
            zonal = -(east - pltpu.roll(east, 1, 0))
            per_cos = by_lat(
                [1.0 / math.sin((min(g, n_lat - 1 - g) + 0.5) * math.pi / n_lat) for g in faces]
            )
            advanced.append(row + zonal - (weighted - below) * per_cos)
        below = weighted
    out_ref[...] = jnp.swapaxes(jnp.stack(advanced), 0, 1)[:n_cols]

    @pl.when(polar)
    def _():
        for step in range(1, lon_count):
            row_copy(step).wait_send()
            line_copy(step).wait_send()
        edge_ce.wait_send()

        @pl.when(is_edge)
        def _():
            for lon in range(lon_count):
                edge_copy(lon).wait_send()

        @pl.when(is_pole)
        def _():
            for step in range(1, lon_count):
                pole_copy(step).wait_send()

    @pl.when(jnp.logical_not(polar))
    def _():
        edge_east.wait_send()
        edge_west.wait_send()
        raw_south.wait_send()
        raw_north.wait_send()

    @pl.when(a < lat_count - 1)
    def _():
        cn_copy.wait_send()


def local_fused(state, courant_east, courant_north, cutoff, filter_mask):
    n_rows, n_cols, n_comp = state.shape
    wide = spread(n_cols)
    synth, analyse, n_waves = wave_tables(n_cols, n_rows, n_rows * 4)
    flat = [
        jnp.transpose(x, (1, 0, 2))
        for x in (state, courant_east, courant_north)
    ]
    vmem = pl.BlockSpec(memory_space=pltpu.VMEM)
    block = pltpu.VMEM((n_rows, wide, n_comp), jnp.float32)
    dma = pltpu.SemaphoreType.DMA
    plane = pltpu.VMEM(flat[0].shape, jnp.float32)
    table = lambda value: pltpu.VMEM(value.shape, jnp.float32)
    edge = lambda count: pltpu.VMEM((count, n_rows, n_comp), jnp.float32)
    result = pl.pallas_call(
        functools.partial(fused_kernel, n_waves),
        out_shape=jax.ShapeDtypeStruct(flat[0].shape, jnp.float32),
        in_specs=[pl.BlockSpec(memory_space=pltpu.HBM)] * 7,
        out_specs=vmem,
        scratch_shapes=[
            pltpu.SMEM(cutoff.shape, jnp.int32), pltpu.SMEM(cutoff.shape, jnp.int32),
            plane, plane, plane, table(synth), table(analyse), dma((7,)),
            block, block, block,
            pltpu.VMEM((n_rows + 4, wide, n_comp), jnp.float32),
            block, block, edge(3), edge(2), edge(3), edge(2),
            pltpu.VMEM((wide, n_comp), jnp.float32),
            dma((n_rows,)), dma((n_rows,)), dma((n_rows,)), dma((n_rows + 4,)), dma((n_rows,)),
            dma((2,)), dma((2,)), dma, dma, dma((2,)), dma((2,)),
        ],
        compiler_params=pltpu.CompilerParams(
            collective_id=0, has_side_effects=True
        ),
    )(cutoff, filter_mask, *flat, synth, analyse)
    return jnp.transpose(result, (1, 0, 2))


def solution(mesh):
    placed = (
        P("lat", "lon", None),
        P("lat", "lon", None),
        P("lat", "lon", None),
        P("lat"),
        P("lat"),
    )

    def dispatch(*arrays):
        n_rows = arrays[0].shape[0]
        row_each = mesh.shape["lat"] == 4 and mesh.shape["lon"] == n_rows and n_rows >= 8
        return (local_fused if row_each else local)(*arrays)

    return jax.shard_map(
        dispatch, mesh=mesh, in_specs=placed, out_specs=P("lat", "lon", None), check_vma=False
    )
```

```python
import functools
import math

import jax
import jax.numpy as jnp
import numpy as np
from jax import lax
from jax.experimental import pallas as pl
from jax.experimental.pallas import tpu as pltpu
from jax.sharding import PartitionSpec as P

HIGHEST = lax.Precision.HIGHEST


def passed_along(block, axis, distance):
    devices = range(lax.axis_size(axis))
    route = [((i - distance) % len(devices), i) for i in devices]
    return lax.ppermute(block, axis, route)


def padded_2(value, sides, width):
    for axis, dim in sides:
        count, length = (lax.axis_size(axis), value.shape[dim])
        up = [(i, (i + 1) % count) for i in range(count)]
        down = [(j, i) for i, j in up]
        last = lax.slice_in_dim(value, length - width, length, axis=dim)
        initial = lax.slice_in_dim(value, 0, width, axis=dim)
        before = lax.ppermute(last, axis, up)
        after = lax.ppermute(initial, axis, down)
        value = jnp.concatenate([before, value, after], axis=dim)
    return value


def face_flux(far_lo, near_lo, near_hi, far_hi, courant):
    centred = (7.0 * (near_lo + near_hi) - (far_lo + far_hi)) / 12.0
    return courant * centred - 0.5 * jnp.abs(courant) * (near_hi - near_lo)


def build_table(n_full, n_half):
    points = jnp.arange(n_full, dtype=jnp.int32)
    waves = jnp.arange(n_half, dtype=jnp.int32)
    phase = points[:, None] * waves[None, :] % n_full
    angle = phase.astype(jnp.float32) * (2.0 * math.pi / n_full)
    return jnp.concatenate([jnp.cos(angle), jnp.sin(angle)], axis=1)


def pole_rows(field):
    return jnp.concatenate([field[:2][::-1], field[::-1][:2]], axis=0)


def send_rows(field):
    return lax.all_to_all(field, "lon", split_axis=2, concat_axis=1, tiled=True)


def return_rows(merged, lon_count):
    smooth = lax.all_to_all(merged, "lon", split_axis=1, concat_axis=2, tiled=True)
    partner = passed_along(pole_rows(smooth), "lon", lon_count // 2)
    return (smooth, partner)


def local(state, courant_east, courant_north, cutoff, filter_mask):
    n_rows, n_cols, n_comp = state.shape
    lon_count = lax.axis_size("lon")
    lat_count = lax.axis_size("lat")
    lat_index = lax.axis_index("lat")
    n_full = n_cols * lon_count
    n_half = n_full // 2 + 1
    n_lat = n_rows * lat_count
    fourier = build_table(n_full, n_half)
    waves = jnp.arange(n_half, dtype=jnp.int32)
    weights = jnp.where((waves == 0) | (waves == n_half - 1), 1.0 / n_full, 2.0 / n_full).astype(
        jnp.float32
    )
    row_lines = send_rows(state)
    kept = jnp.where(waves[None, :] <= cutoff[:, None], weights[None, :], 0.0)
    kept_both = jnp.concatenate([kept, kept], axis=1)
    coeffs = lax.dot_general(
        row_lines, fourier, (((1,), (0,)), ((), ())), precision=lax.Precision.HIGHEST
    )
    coeffs = coeffs * kept_both[:, None, :]
    synth = lax.dot_general(
        coeffs, fourier, (((2,), (1,)), ((), ())), precision=lax.Precision.HIGHEST
    )
    filtered = jnp.transpose(synth, (0, 2, 1))
    merged = jnp.where(filter_mask[:, None, None] == 1, filtered, row_lines)
    smooth, partner = return_rows(merged, lon_count)
    stacked = jnp.stack([smooth, courant_east, courant_north])
    padded = padded_2(stacked, (("lat", 1), ("lon", 2)), 2)
    zonal_p = padded[0, 2:-2]
    zonal_c = padded[1, 2:-2]
    east = face_flux(
        zonal_p[:, 0 : n_cols + 1],
        zonal_p[:, 1 : n_cols + 2],
        zonal_p[:, 2 : n_cols + 3],
        zonal_p[:, 3 : n_cols + 4],
        zonal_c[:, 1 : n_cols + 2],
    )
    zonal = -(east[:, 1:] - east[:, :-1])
    merid_p = padded[0, :, 2:-2]
    south = jnp.where(lat_index == 0, partner[:2], merid_p[:2])
    north = jnp.where(lat_index == lat_count - 1, partner[2:], merid_p[-2:])
    merid_p = jnp.concatenate([south, merid_p[2:-2], north], axis=0)
    merid_c = padded[2, :, 2:-2]
    north_flux = face_flux(
        merid_p[0 : n_rows + 1],
        merid_p[1 : n_rows + 2],
        merid_p[2 : n_rows + 3],
        merid_p[3 : n_rows + 4],
        merid_c[1 : n_rows + 2],
    )
    face_rows = lat_index * n_rows + jnp.arange(-1, n_rows, dtype=jnp.int32)
    cos_face = jnp.sin(
        jnp.minimum(face_rows + 1, n_lat - 1 - face_rows).astype(jnp.float32) * (math.pi / n_lat)
    )
    cell_rows = face_rows[1:]
    cos_cell = jnp.sin(
        (jnp.minimum(cell_rows, n_lat - 1 - cell_rows).astype(jnp.float32) + 0.5)
        * (math.pi / n_lat)
    )
    weighted = cos_face[:, None, None] * north_flux
    meridional = -(weighted[1:] - weighted[:-1]) / cos_cell[:, None, None]
    return smooth + zonal + meridional


def spread(n_cols):
    return -(-(n_cols + 4) // 8) * 8


def wave_tables(n_cols, lon_count, n_lat):
    n_full, wide = n_cols * lon_count, spread(n_cols)
    low = n_full // 8
    n_waves = low + (n_full // 2 - 1 - low) * (n_lat // 4 - 1) // (n_lat // 2) + 1
    lanes = -(-2 * n_waves // 128) * 128
    place = np.arange(wide)
    offset = np.where(place < n_cols + 2, place, place - wide)
    column = (np.arange(lon_count)[:, None] * n_cols + offset[None, :]).reshape(-1) % n_full
    angle = column[:, None] * np.arange(n_waves)[None, :] % n_full * (2.0 * np.pi / n_full)
    table = np.zeros((lon_count * wide, lanes), np.float64)
    table[:, : 2 * n_waves] = np.concatenate([np.cos(angle), np.sin(angle)], axis=1)
    given = np.tile((place < n_cols + 2) | (place >= wide - 2), lon_count)
    own = np.tile(place < n_cols, lon_count)
    synth = np.where(given[:, None], table, 0.0).astype(np.float32)
    analyse = np.where(own[:, None], table, 0.0).T.astype(np.float32)
    return synth, analyse, n_waves


def fused_kernel(
    n_waves, cut_in, mask_in, st_in, ce_in, cn_in, t1_in, t2_in, out_ref,
    cut_ref, mask_ref, st_ref, ce_ref, cn_ref, t1_ref, t2_ref, loaded,
    blocks, lines, synth, ext, ce_rows, cn_rows, to_east, to_west, from_west, from_east, cn_south,
    send_a, recv_a, send_b, recv_rows, send_c, send_raw, recv_raw, send_cn, recv_cn,
    send_edge, recv_edge,
):
    n_rows, wide, n_comp = blocks.shape
    n_cols = st_ref.shape[0]
    n_full = n_rows * n_cols
    lat_count, lon_count = lax.axis_size("lat"), n_rows
    n_lat = n_rows * lat_count
    a, i = lax.axis_index("lat"), lax.axis_index("lon")
    southern = a < 2
    polar = jnp.logical_or(a == 0, a == lat_count - 1)
    other = jnp.where(southern, 1 - a, 5 - a)
    first_edge = jnp.where(southern, n_rows - 2, 0)
    first_pole = jnp.where(southern, 0, n_rows - 2)
    is_edge = jnp.logical_and(i >= first_edge, i < first_edge + 2)
    is_pole = jnp.logical_and(i >= first_pole, i < first_pole + 2)
    east_i, west_i = lax.rem(i + 1, lon_count), lax.rem(i + lon_count - 1, lon_count)
    half = lon_count // 2

    def remote(src, dst, send, recv, lat, lon):
        return pltpu.make_async_remote_copy(
            src_ref=src, dst_ref=dst, send_sem=send, recv_sem=recv,
            device_id=(lat, lon), device_id_type=pl.DeviceIdType.MESH,
        )

    loads = [
        pltpu.make_async_copy(src, dst, loaded.at[k])
        for k, (src, dst) in enumerate(
            [
                (st_in, st_ref), (ce_in, ce_ref), (cn_in, cn_ref), (t1_in, t1_ref),
                (t2_in, t2_ref), (cut_in, cut_ref), (mask_in, mask_ref),
            ]
        )
    ]
    for load in loads:
        load.start()
    barrier = pltpu.get_barrier_semaphore()

    def greet(lat, lon):
        pl.semaphore_signal(
            barrier, inc=1, device_id=(lat, lon), device_id_type=pl.DeviceIdType.MESH
        )

    @pl.when(polar)
    def _():
        for step in range(1, lon_count):
            greet(a, lax.rem(i + step, lon_count))

        @pl.when(is_edge)
        def _():
            for lon in range(lon_count):
                greet(other, lon)

        @pl.when(jnp.logical_not(is_edge))
        def _():
            greet(other, i)

    @pl.when(jnp.logical_not(polar))
    def _():
        greet(a, east_i)
        greet(a, west_i)
        greet(3 - a, i)
        greet(other, first_edge)
        greet(other, first_edge + 1)

        @pl.when(jnp.logical_not(is_edge))
        def _():
            greet(other, i)

    loads[0].wait()
    pad = jnp.zeros((wide - n_cols, n_rows, n_comp), jnp.float32)

    def rows_first(ref):
        return jnp.swapaxes(jnp.concatenate([ref[...], pad], axis=0), 0, 1)

    blocks[...] = rows_first(st_ref)

    @pl.when(jnp.logical_not(polar))
    def _():
        to_east[0] = st_ref[n_cols - 2]
        to_east[1] = st_ref[n_cols - 1]
        to_west[0] = st_ref[0]
        to_west[1] = st_ref[1]

    @pl.when(polar)
    def _():
        lines[i] = blocks[i]

    @pl.when(a == 0)
    def _():
        cn_south[...] = jnp.zeros_like(cn_south)

    @pl.when(polar)
    def _():
        pl.semaphore_wait(barrier, lon_count - 1 + jnp.where(is_edge, lon_count, 1))

    @pl.when(jnp.logical_not(polar))
    def _():
        pl.semaphore_wait(barrier, 5 + jnp.where(is_edge, 0, 1))

    order = sorted(range(1, lon_count), key=lambda step: -abs(step - half))

    def row_copy(step):
        to = lax.rem(i + step, lon_count)
        return remote(blocks.at[to], lines.at[i], send_a.at[step], recv_a.at[step], a, to)

    cn_copy = remote(cn_rows.at[n_rows - 1], cn_south, send_cn, recv_cn, a + 1, i)
    edge_ce = remote(
        to_east.at[2], from_west.at[2], send_edge.at[0], recv_edge.at[0], a, east_i
    )
    edge_east = remote(to_east, from_west, send_edge.at[0], recv_edge.at[0], a, east_i)
    edge_west = remote(to_west, from_east, send_edge.at[1], recv_edge.at[1], a, west_i)
    raw_south = remote(
        blocks.at[pl.ds(0, 2)], ext.at[pl.ds(n_rows + 2, 2)],
        send_raw.at[0], recv_raw.at[1], a - 1, i,
    )
    raw_north = remote(
        blocks.at[pl.ds(n_rows - 2, 2)], ext.at[pl.ds(0, 2)],
        send_raw.at[1], recv_raw.at[0], a + 1, i,
    )

    @pl.when(polar)
    def _():
        for step in order:
            row_copy(step).start()

    @pl.when(jnp.logical_not(polar))
    def _():
        edge_west.start()
        raw_south.start()
        raw_north.start()

    for load in loads[1:3]:
        load.wait()
    to_east[2] = ce_ref[n_cols - 1]
    cn_rows[...] = rows_first(cn_ref)

    @pl.when(polar)
    def _():
        edge_ce.start()

    @pl.when(jnp.logical_not(polar))
    def _():
        edge_east.start()

    @pl.when(a < lat_count - 1)
    def _():
        cn_copy.start()

    def line_copy(step):
        to = lax.rem(i + step, lon_count)
        return remote(
            synth.at[to], ext.at[i + 2], send_b.at[step], recv_rows.at[i + 2], a, to
        )

    pole_slot = jnp.where(southern, 1 - i, n_rows * 2 + 1 - i)
    edge_slot = jnp.where(southern, i - (n_rows - 2), n_rows + 2 + i)

    def pole_copy(step):
        to = lax.rem(i + step, lon_count)
        return remote(
            synth.at[lax.rem(to + half, lon_count)], ext.at[pole_slot],
            send_c.at[step], recv_rows.at[pole_slot], a, to,
        )

    def edge_copy(lon):
        return remote(
            synth.at[lon], ext.at[edge_slot], send_c.at[lon], recv_rows.at[edge_slot], other, lon
        )

    def slot_wait(slot):
        remote(blocks.at[0], ext.at[slot], send_b.at[0], recv_rows.at[slot], a, east_i).wait_recv()

    ce_rows[...] = rows_first(ce_ref)
    for load in loads[3:]:
        load.wait()

    @pl.when(polar)
    def _():
        lane = lax.broadcasted_iota(jnp.int32, (1, t1_ref.shape[1]), 1)
        wave = jnp.where(lane < n_waves, lane, lane - n_waves)
        kept = jnp.where(wave == 0, 1.0 / n_full, 2.0 / n_full).astype(jnp.float32)
        kept = jnp.where(wave <= cut_ref[i], kept, 0.0)
        weights = lax.dot_general(
            t1_ref[...] * kept, t2_ref[...], (((1,), (0,)), ((), ())), precision=HIGHEST,
            preferred_element_type=jnp.float32,
        )
        size = lon_count * wide
        dim = (lon_count, wide, 1)
        place = lax.broadcasted_iota(jnp.int32, dim, 1)
        at = lax.broadcasted_iota(jnp.int32, dim, 0) * n_cols
        at = at + jnp.where(place < n_cols + 2, place, place - wide)
        at = jnp.where(at < 0, at + n_full, jnp.where(at >= n_full, at - n_full, at))
        at = jnp.where((place >= n_cols + 2) & (place < wide - 2), -1, at).reshape(size, 1)
        lane = lax.broadcasted_iota(jnp.int32, (1, size), 1)
        start = jnp.zeros((1, size), jnp.int32)
        for q in range(1, lon_count):
            start = start + jnp.where(lane >= q * wide, 1, 0)
        inner = lane - start * wide
        source = jnp.where(inner < n_cols, start * n_cols + inner, -2)
        weights = jnp.where(mask_ref[i] == 1, weights, jnp.where(at == source, 1.0, 0.0))
        w_hi = weights.astype(jnp.bfloat16)
        w_lo = (weights - w_hi.astype(jnp.float32)).astype(jnp.bfloat16)
        for step in range(1, lon_count):
            row_copy(step).wait_recv()
        line = lines[...].reshape(size, n_comp)
        l_hi = line.astype(jnp.bfloat16)
        l_lo = (line - l_hi.astype(jnp.float32)).astype(jnp.bfloat16)

        def times(left, right):
            return lax.dot_general(
                left, right, (((1,), (0,)), ((), ())), preferred_element_type=jnp.float32
            )

        smooth = times(w_hi, l_hi) + (times(w_hi, l_lo) + times(w_lo, l_hi))
        synth[...] = smooth.reshape(lon_count, wide, n_comp)
        for step in order:
            line_copy(step).start()

        @pl.when(is_edge)
        def _():
            for lon in range(lon_count):
                edge_copy(lon).start()

        @pl.when(is_pole)
        def _():
            for step in order:
                pole_copy(step).start()
            ext[pole_slot] = synth[lax.rem(i + half, lon_count)]

        ext[i + 2] = synth[i]

    @pl.when(jnp.logical_not(polar))
    def _():
        edge_east.wait_recv()
        edge_west.wait_recv()
        place = lax.broadcasted_iota(jnp.int32, (wide, 1), 0)
        for r in range(n_rows):
            row = blocks[r]
            row = jnp.where(place == wide - 2, from_west[0, r : r + 1, :], row)
            row = jnp.where(place == wide - 1, from_west[1, r : r + 1, :], row)
            row = jnp.where(place == n_cols, from_east[0, r : r + 1, :], row)
            row = jnp.where(place == n_cols + 1, from_east[1, r : r + 1, :], row)
            ext[r + 2] = row

    @pl.when(polar)
    def _():
        edge_ce.wait_recv()

    @pl.when(a > 0)
    def _():
        cn_copy.wait_recv()

    @pl.when(southern)
    def _():
        raw_south.wait_recv()

    @pl.when(jnp.logical_not(southern))
    def _():
        raw_north.wait_recv()

    @pl.when(polar)
    def _():
        for step in range(1, lon_count):
            slot_wait(lax.rem(i + step, lon_count) + 2)
        for m in range(2):
            owner = first_pole + m
            slot = jnp.where(southern, 1 - m, n_rows + 3 - m)

            @pl.when(owner != i)
            def _():
                slot_wait(slot)

    @pl.when(jnp.logical_not(polar))
    def _():
        for m in range(2):
            slot_wait(jnp.where(southern, m, n_rows + 2 + m))

    def by_lat(values):
        chosen = jnp.float32(values[0])
        for lat in range(1, lat_count):
            chosen = jnp.where(a == lat, jnp.float32(values[lat]), chosen)
        return chosen

    def flux(far_lo, near_lo, near_hi, far_hi, courant):
        centred = (7.0 * (near_lo + near_hi) - (far_lo + far_hi)) * (1.0 / 12.0)
        return courant * centred - 0.5 * jnp.abs(courant) * (near_hi - near_lo)

    place = lax.broadcasted_iota(jnp.int32, (wide, 1), 0)
    below, advanced = None, []
    for f in range(-1, n_rows):
        faces = [lat * n_rows + f for lat in range(lat_count)]
        cos_face = by_lat([math.sin(min(g + 1, n_lat - 1 - g) * math.pi / n_lat) for g in faces])
        courant = cn_south[...] if f < 0 else cn_rows[f]
        stencil = [ext[f + 1 + t] for t in range(4)]
        weighted = cos_face * flux(*stencil, courant)
        if f >= 0:
            row = ext[f + 2]
            u = jnp.where(place == wide - 1, from_west[2, f : f + 1, :], ce_rows[f])
            east = flux(
                pltpu.roll(row, 1, 0), row, pltpu.roll(row, wide - 1, 0),
                pltpu.roll(row, wide - 2, 0), u,
            )
            zonal = -(east - pltpu.roll(east, 1, 0))
            per_cos = by_lat(
                [1.0 / math.sin((min(g, n_lat - 1 - g) + 0.5) * math.pi / n_lat) for g in faces]
            )
            advanced.append(row + zonal - (weighted - below) * per_cos)
        below = weighted
    out_ref[...] = jnp.swapaxes(jnp.stack(advanced), 0, 1)[:n_cols]

    @pl.when(polar)
    def _():
        for step in range(1, lon_count):
            row_copy(step).wait_send()
            line_copy(step).wait_send()
        edge_ce.wait_send()

        @pl.when(is_edge)
        def _():
            for lon in range(lon_count):
                edge_copy(lon).wait_send()

        @pl.when(is_pole)
        def _():
            for step in range(1, lon_count):
                pole_copy(step).wait_send()

    @pl.when(jnp.logical_not(polar))
    def _():
        edge_east.wait_send()
        edge_west.wait_send()
        raw_south.wait_send()
        raw_north.wait_send()

    @pl.when(a < lat_count - 1)
    def _():
        cn_copy.wait_send()


def local_fused(state, courant_east, courant_north, cutoff, filter_mask):
    n_rows, n_cols, n_comp = state.shape
    wide = spread(n_cols)
    synth, analyse, n_waves = wave_tables(n_cols, n_rows, n_rows * 4)
    flat = [
        jnp.transpose(x, (1, 0, 2))
        for x in (state, courant_east, courant_north)
    ]
    vmem = pl.BlockSpec(memory_space=pltpu.VMEM)
    block = pltpu.VMEM((n_rows, wide, n_comp), jnp.float32)
    dma = pltpu.SemaphoreType.DMA
    plane = pltpu.VMEM(flat[0].shape, jnp.float32)
    table = lambda value: pltpu.VMEM(value.shape, jnp.float32)
    edge = lambda count: pltpu.VMEM((count, n_rows, n_comp), jnp.float32)
    result = pl.pallas_call(
        functools.partial(fused_kernel, n_waves),
        out_shape=jax.ShapeDtypeStruct(flat[0].shape, jnp.float32),
        in_specs=[pl.BlockSpec(memory_space=pltpu.HBM)] * 7,
        out_specs=vmem,
        scratch_shapes=[
            pltpu.SMEM(cutoff.shape, jnp.int32), pltpu.SMEM(cutoff.shape, jnp.int32),
            plane, plane, plane, table(synth), table(analyse), dma((7,)),
            block, block, block,
            pltpu.VMEM((n_rows + 4, wide, n_comp), jnp.float32),
            block, block, edge(3), edge(2), edge(3), edge(2),
            pltpu.VMEM((wide, n_comp), jnp.float32),
            dma((n_rows,)), dma((n_rows,)), dma((n_rows,)), dma((n_rows + 4,)), dma((n_rows,)),
            dma((2,)), dma((2,)), dma, dma, dma((2,)), dma((2,)),
        ],
        compiler_params=pltpu.CompilerParams(
            collective_id=0, has_side_effects=True
        ),
    )(cutoff, filter_mask, *flat, synth, analyse)
    return jnp.transpose(result, (1, 0, 2))


def solution(mesh):
    placed = (
        P("lat", "lon", None),
        P("lat", "lon", None),
        P("lat", "lon", None),
        P("lat"),
        P("lat"),
    )

    def dispatch(*arrays):
        n_rows = arrays[0].shape[0]
        row_each = mesh.shape["lat"] == 4 and mesh.shape["lon"] == n_rows and n_rows >= 8
        return (local_fused if row_each else local)(*arrays)

    return jax.shard_map(
        dispatch, mesh=mesh, in_specs=placed, out_specs=P("lat", "lon", None), check_vma=False
    )
```
